128 devices in a mesh: dp: 2 (over y_hi), fsdp: 16 (over z, x), tensor: 4 (over y_lo, core).
Axes of the slice: x: 4, y: 4 (y_hi: 2, y_lo: 2; y = y_hi * 2 + y_lo), z: 4, core: 2. Of those that a mesh axis runs over, the one named last changes fastest.
Arguments:
- activations: bfloat16 [512, 8192], P('dp', 'fsdp'), may hold values from -6 to 6
- frozen_weight: bfloat16 [8192, 28672], P('fsdp', 'tensor'), may hold values from -0.0625 to 0.0625
- cayley_params: float32 [4, 256, 1024], replicated, may hold values from -0.9 to 0.9
- permutations: int32 [4, 8192], replicated, may hold values from 0 to 8191, as said below
- cotangent: bfloat16 [512, 28672], P('dp', 'tensor'), may hold values from -6 to 6
Outputs:
- projected: bfloat16 [512, 28672], P(('dp', 'fsdp'), 'tensor')
- param_grads: float32 [4, 256, 1024], P(None, ('dp', 'fsdp'))
The draws below stay inside these ranges and needn't reach their ends.
Inputs may be any that keep to these rules, and one draw needn't show every extreme that they name: Row k is a butterfly permutation with span S = 8192 / 2^(3 - k): for position p = q * 32 + i, with q the block and i < 32, permutations[k, p] = (p - p mod S) + h * S / 2 + (q mod (S / 32)) * 16 + r, where h = sigma(i) // 16 and r = sigma(i) mod (16), and sigma is a permutation of 0 to 31 chosen for each factor and block.
All inputs are finite; a program needn't handle non-finite values.
Results may differ from the reference program's by a relative error of at most 0.012.
Values may be sent and summed in bfloat16 or wider, within the bound.
No kernel may reach another device: no remote copies, remote signals or barrier semaphores. Data moves between devices by JAX's collectives and lax.ppermute only.
A program may use at most 192 MiB of HBM per device.

```python
import jax
import jax.numpy as jnp
from jax import lax

D = 8192
FF = 28672
BLOCK = 32
FACTORS = 4
TOKENS = 512
BLOCKS = 256


def draw_permutations(key, part):
    key = jax.random.fold_in(key, 11)
    halfway = BLOCK // 2
    subkeys = jax.random.split(key, FACTORS * BLOCKS)
    shuffles = jax.vmap(lambda single: jax.random.permutation(single, BLOCK))(subkeys).astype(jnp.int32)
    shuffles = shuffles.reshape(FACTORS, D)
    position = jnp.arange(D, dtype=jnp.int32)
    blocknum = position // BLOCK
    tables = []
    for factor in range(FACTORS):
        extent = D // 2 ** (FACTORS - 1 - factor)
        sigma = shuffles[factor]
        halves = sigma // halfway
        residue = sigma % halfway
        anchor = position // extent * extent
        source = anchor + halves * (extent // 2) + blocknum % (extent // BLOCK) * halfway + residue
        tables.append(source.astype(jnp.int32))
    return jnp.stack(tables).astype(jnp.int32)


def signed_vector(key, shape):
    first, second = jax.random.split(key)
    magnitude = jax.random.uniform(first, shape, jnp.float32, 0.7, 1.0)
    signs = (2 * jax.random.randint(second, shape, 0, 2) - 1).astype(jnp.float32)
    return magnitude * signs


def draw_cayley_params(key, part):
    key = jax.random.fold_in(key, 23)
    key_left, key_right, key_noise, key_scale = jax.random.split(key, 4)
    strength = 0.6
    rough = 0.3
    left = signed_vector(key_left, (FACTORS, BLOCKS, BLOCK, 1))
    right = signed_vector(key_right, (FACTORS, BLOCKS, 1, BLOCK))
    block_scale = jax.random.uniform(key_scale, (FACTORS, BLOCKS, 1, 1), jnp.float32, 0.5, 1.0)
    noise = jax.random.uniform(key_noise, (FACTORS, BLOCKS, BLOCK, BLOCK), jnp.float32, -rough, rough)
    values = strength * block_scale * left * right + noise
    values = jnp.clip(values, -0.9, 0.9)
    return values.reshape(FACTORS, BLOCKS, BLOCK * BLOCK).astype(jnp.float32)


def shard_levels(stream_key, dims, cuts, low, high):
    level = 1.0
    for dim, shards_of in cuts:
        draws = jax.random.uniform(jax.random.fold_in(jax.random.fold_in(stream_key, 6), dim), (shards_of,), jnp.float32, low / len(cuts), high / len(cuts))
        level = level * jnp.repeat(jnp.exp(draws), dims[dim] // shards_of).reshape((-1,) + (1,) * (len(dims) - 1 - dim))
    return level


def gaussian(own_key, dims, scale, most, cuts=(), kind=jnp.bfloat16):
    gain = shard_levels(own_key, dims, cuts, -0.22, 0.18) if cuts else 1.0
    drawn = jax.random.normal(own_key, dims, jnp.float32) * scale * gain
    return jnp.minimum(jnp.maximum(drawn, -most), most).astype(kind)


def setup_inputs(seed: int = 0) -> dict:
    seeds = jax.random.split(jax.random.key(seed), 6)
    return {
        "activations": gaussian(seeds[0], (TOKENS, D), 1.0, 6.0, ((0, 2), (1, 16))),
        "frozen_weight": gaussian(seeds[1], (D, FF), D ** -0.5, 0.0625, ((0, 16), (1, 4))),
        "cayley_params": draw_cayley_params(jax.random.fold_in(seeds[5], 71), 0),
        "permutations": draw_permutations(jax.random.fold_in(seeds[5], 71), 0),
        "cotangent": gaussian(seeds[4], (TOKENS, FF), 1.0, 6.0, ((0, 2), (1, 4))),
    }


HI = lax.Precision.HIGHEST

def cayley(params):
    shaped = params.reshape(params.shape[0], params.shape[1], BLOCK, BLOCK)
    skew = shaped - jnp.swapaxes(shaped, 2, 3)
    ident = jnp.eye(BLOCK, dtype=jnp.float32)
    plus = ident + skew
    metric = ident - jnp.matmul(skew, skew, precision=HI)
    right = jnp.matmul(plus, plus, precision=HI)
    lower = jnp.linalg.cholesky(metric)
    half = jax.scipy.linalg.solve_triangular(lower, right, lower=True)
    return jax.scipy.linalg.solve_triangular(lower, half, lower=True, trans=1)

def reference(activations, frozen_weight, cayley_params, permutations, cotangent):
    rotation = cayley(cayley_params)
    rotation_half = rotation.astype(jnp.bfloat16).astype(jnp.float32)
    count = activations.shape[0]
    state = activations
    moved_list = []
    for level in range(FACTORS):
        moved = jnp.take(state, permutations[level], axis=1)
        moved_list.append(moved)
        shaped = moved.astype(jnp.float32).reshape(count, BLOCKS, BLOCK)
        state = jnp.einsum('tbi,bij->tbj', shaped, rotation_half[level], precision=HI).reshape(count, D).astype(jnp.bfloat16)
    projected = jnp.dot(state.astype(jnp.float32), frozen_weight.astype(jnp.float32), preferred_element_type=jnp.float32).astype(jnp.bfloat16)
    upstream = lax.dot_general(cotangent.astype(jnp.float32), frozen_weight.astype(jnp.float32), (((1,), (1,)), ((), ())), preferred_element_type=jnp.float32).astype(jnp.bfloat16)
    grads = [None] * FACTORS
    for level in reversed(range(FACTORS)):
        up_blocks = upstream.astype(jnp.float32).reshape(count, BLOCKS, BLOCK)
        moved_blocks = moved_list[level].astype(jnp.float32).reshape(count, BLOCKS, BLOCK)
        grads[level] = jnp.einsum('tbi,tbj->bij', moved_blocks, up_blocks, precision=HI)
        if level > 0:
            spread = jnp.einsum('tbj,bij->tbi', up_blocks, rotation_half[level], precision=HI).reshape(count, D).astype(jnp.bfloat16)
            upstream = jnp.zeros_like(spread).at[:, permutations[level]].set(spread)
    block_grad = jnp.stack(grads)
    _, pull = jax.vjp(cayley, cayley_params)
    param_grads = pull(block_grad)[0]
    return (projected, param_grads)
```

```python
import functools

import jax
import jax.numpy as jnp
from jax import lax
from jax.experimental import pallas as pl
from jax.experimental.pallas import tpu as pltpu
from jax.sharding import PartitionSpec as P

BLOCK = 32
FACTORS = 4
RUN = 16
LANES = 128
BF = jnp.bfloat16
F32 = jnp.float32
HI = lax.Precision.HIGHEST


def iota(shape, dim):
    return lax.broadcasted_iota(jnp.int32, shape, dim)


def dot(a, b, ca, cb, precision=None):
    return lax.dot_general(
        a, b, (((ca,), (cb,)), ((), ())), precision=precision, preferred_element_type=F32
    )


def call(body, out_shape, args, scratch=(), limit=48 << 20):
    return pl.pallas_call(
        body,
        out_shape=out_shape,
        in_specs=[pl.BlockSpec(memory_space=pltpu.VMEM)] * len(args),
        out_specs=jax.tree.map(lambda _: pl.BlockSpec(memory_space=pltpu.VMEM), out_shape),
        scratch_shapes=list(scratch),
        compiler_params=pltpu.CompilerParams(vmem_limit_bytes=limit),
    )(*args)


def shape(dims, dtype):
    return jax.ShapeDtypeStruct(dims, dtype)


def inverse_body(p_ref, rd_ref, ad_ref, turned, mat, rows):
    turned[...] = p_ref[...].T
    sub = iota((BLOCK, LANES), 0)
    for i in range(BLOCK):
        skew = turned[i * BLOCK : (i + 1) * BLOCK, :] - turned[pl.ds(i, BLOCK, stride=BLOCK), :]
        mat[i] = jnp.where(sub == i, 1.0, 0.0) - skew

    def step(k, carry):
        here = sub == k
        pivot = 1.0 / mat[k, pl.ds(k, 1), :]
        line = jnp.where(here, pivot, mat[k] * pivot)
        for i in range(BLOCK):
            factor = mat[i, pl.ds(k, 1), :]
            mat[i] = jnp.where(here, 0.0, mat[i]) - factor * line
        mat[k] = line
        return carry

    lax.fori_loop(0, BLOCK, step, 0)
    for i in range(BLOCK):
        rows[pl.ds(i, LANES, stride=BLOCK), :] = mat[i].T
    same = iota((LANES, LANES), 0) // BLOCK == iota((LANES, LANES), 1) // BLOCK
    unit = jnp.where(iota((LANES, LANES), 0) == iota((LANES, LANES), 1), 1.0, 0.0)
    for g in range(24):
        piece = rows[g * LANES : (g + 1) * LANES, :]
        wide = jnp.where(same, jnp.concatenate([piece] * 4, axis=1), 0.0)
        if g < 16:
            rd_ref[g * LANES : (g + 1) * LANES, :] = (2.0 * wide - unit).astype(BF)
        else:
            ad_ref[(g - 16) * LANES : (g - 15) * LANES, :] = wide


def onehot(idx_ref, level, g):
    return jnp.where(
        iota((LANES, LANES), 0) == idx_ref[level : level + 1, g * LANES : (g + 1) * LANES], 1.0, 0.0
    ).astype(BF)


def shuffle(x, level):
    groups = 16 >> level
    width = 512 // groups
    pieces = []
    for h in range(groups // 2):
        for i in range(width // RUN):
            for half in range(2):
                start = (2 * h + half) * width + i * RUN
                pieces.append(x[start : start + RUN])
    return jnp.concatenate(pieces, axis=0)


def unshuffle(x, level):
    groups = 16 >> level
    width = 512 // groups
    count = width // RUN
    pieces = []
    for a in range(groups):
        for i in range(count):
            start = ((a // 2) * count + i) * BLOCK + (a % 2) * RUN
            pieces.append(x[start : start + RUN])
    return jnp.concatenate(pieces, axis=0)


def forward_body(x_ref, rd_ref, idx_ref, out_ref, moved_ref):
    x = x_ref[...]
    for level in range(FACTORS):
        x = shuffle(x, level)
        outs = []
        for g in range(4):
            moved = dot(onehot(idx_ref, level, g), x[g * LANES : (g + 1) * LANES], 0, 0).astype(BF)
            base = (level * 4 + g) * LANES
            moved_ref[base : base + LANES, :] = moved
            rot = rd_ref[base : base + LANES, :]
            if level < FACTORS - 1:
                outs.append(dot(rot, moved, 0, 0).astype(BF))
            else:
                out_ref[:, g * LANES : (g + 1) * LANES] = dot(moved, rot, 0, 0).astype(BF)
        if level < FACTORS - 1:
            x = jnp.concatenate(outs, axis=0)


def backward_body(up_ref, moved_ref, rd_ref, idx_ref, grad_ref):
    up = up_ref[...]
    same = iota((LANES, LANES), 0) // BLOCK == iota((LANES, LANES), 1) // BLOCK
    for level in reversed(range(FACTORS)):
        outs = []
        for g in range(4):
            base = (level * 4 + g) * LANES
            mine = up[g * LANES : (g + 1) * LANES]
            outer = jnp.where(same, dot(moved_ref[base : base + LANES, :], mine, 1, 1), 0.0)
            packed = outer[:BLOCK] + outer[BLOCK : 2 * BLOCK]
            packed = packed + outer[2 * BLOCK : 3 * BLOCK] + outer[3 * BLOCK :]
            grad_ref[level, g] = packed
            if level > 0:
                spread = dot(rd_ref[base : base + LANES, :], mine, 1, 0).astype(BF)
                outs.append(dot(onehot(idx_ref, level, g), spread, 1, 0).astype(BF))
        if level > 0:
            up = unshuffle(jnp.concatenate(outs, axis=0), level)


def pull_body(g_ref, ad_ref, out_ref):
    same = iota((LANES, LANES), 0) // BLOCK == iota((LANES, LANES), 1) // BLOCK
    for g in range(8):
        grad = jnp.where(same, jnp.concatenate([g_ref[g]] * 4, axis=0), 0.0)
        inv = ad_ref[g * LANES : (g + 1) * LANES, :]
        both = 2.0 * dot(dot(inv, grad, 0, 0, HI), inv, 1, 1, HI)
        both = both - both.T
        packed = both[:BLOCK] + both[BLOCK : 2 * BLOCK]
        out_ref[g] = packed + both[2 * BLOCK : 3 * BLOCK] + both[3 * BLOCK :]


def fetch(array, start, count, axis):
    return lax.dynamic_slice_in_dim(array, start, count, axis)


def own_blocks(table, f):
    tail = table.shape[2:]
    parts = []
    for level in range(FACTORS):
        groups = 8 >> level
        shaped = table[level].reshape(groups, 256 // groups, *tail)
        parts.append(fetch(shaped, f * (16 // groups), 16 // groups, 1).reshape(16, *tail))
    return jnp.concatenate(parts, axis=0)


def shift_z(s):
    return [(z * 4 + x, ((z + s) % 4) * 4 + x) for z in range(4) for x in range(4)]


def shift_x(s):
    return [(z * 4 + x, z * 4 + (x + s) % 4) for z in range(4) for x in range(4)]


def send(x, pairs, axis="fsdp"):
    return lax.ppermute(x, axis, pairs)


def roll(x, by, axis):
    return fetch(jnp.concatenate([x, x], axis=axis), by, x.shape[axis], axis)


def reduce_stage(part, shift):
    half = part.shape[1] // 2
    from_low = send(part[2, :half], shift(1))
    from_high = send(part[2, half:], shift(3))
    up = jnp.concatenate([(part[1, :half].astype(F32) + from_low).astype(BF), part[1, half:]], 0)
    down = jnp.concatenate([part[3, :half], (part[3, half:].astype(F32) + from_high).astype(BF)], 0)
    return (part[0].astype(F32) + send(up, shift(1)) + send(down, shift(3))).astype(BF)


def direct_stage(part, shift):
    total = part[0].astype(F32)
    for s in (1, 3, 2):
        total = total + send(part[s], shift(s))
    return total.astype(BF)


def local(activations, frozen_weight, cayley_params, permutations, cotangent):
    f = lax.axis_index("fsdp")
    d = lax.axis_index("dp")
    z, x = f // 4, f % 4
    tokens = activations.shape[0]

    mixed = lax.all_to_all(
        activations.T.reshape(16, BLOCK, tokens), "fsdp", 0, 0, tiled=True
    ).reshape(512, tokens)

    dest = fetch(cayley_params, (d * 16 + f) * 8, 8, 1).reshape(32, BLOCK * BLOCK)
    blocks = jnp.concatenate(
        [own_blocks(cayley_params, f), dest, jnp.zeros((32, BLOCK * BLOCK), F32)], axis=0
    )
    rd, ad = call(
        inverse_body,
        (shape((2048, LANES), BF), shape((1024, LANES), F32)),
        (blocks,),
        (
            pltpu.VMEM((BLOCK * BLOCK, LANES), F32),
            pltpu.VMEM((BLOCK, BLOCK, LANES), F32),
            pltpu.VMEM((BLOCK * LANES, BLOCK), F32),
        ),
    )

    sizes = jnp.array([1024, 2048, 4096, 8192], jnp.int32).reshape(FACTORS, 1)
    sigma = (permutations % sizes) // (sizes // 2) * RUN + permutations % RUN
    idx = own_blocks(sigma.reshape(FACTORS, 256, BLOCK), f).reshape(FACTORS, 512)
    idx = idx + (jnp.arange(512, dtype=jnp.int32) // BLOCK % 4 * BLOCK)[None]

    state, moved = call(
        forward_body, (shape((tokens, 512), BF), shape((2048, tokens), BF)), (mixed, rd, idx)
    )

    state = roll(roll(state.reshape(4, 4, RUN, 512), z, 0), x, 1)
    half = frozen_weight.shape[1] // 2
    first = jnp.dot(
        state.reshape(tokens, 512), frozen_weight[:, :half], preferred_element_type=F32
    ).astype(BF)
    second = jnp.dot(
        state.transpose(1, 0, 2, 3).reshape(tokens, 512),
        frozen_weight[:, half:],
        preferred_element_type=F32,
    ).astype(BF)
    first = reduce_stage(first.reshape(4, 64, half), shift_z)
    second = reduce_stage(second.reshape(4, 64, half), shift_x)
    first = direct_stage(first.reshape(4, RUN, half), shift_x)
    second = direct_stage(second.reshape(4, RUN, half), shift_z)
    projected = jnp.concatenate([first, second], axis=1)

    up = dot(frozen_weight, cotangent, 1, 1).astype(BF)
    up = (up.astype(F32) + send(up, [(t, t ^ 1) for t in range(4)], "tensor")).astype(BF)
    up = (up.astype(F32) + send(up, [(t, t ^ 2) for t in range(4)], "tensor")).astype(BF)

    grads = call(
        backward_body, shape((FACTORS, 4, BLOCK, LANES), F32), (up, moved, rd, idx)
    )
    grads = fetch(grads, 2 * d, 2, 1) + send(
        fetch(grads, 2 - 2 * d, 2, 1), [(0, 1), (1, 0)], "dp"
    )

    low, high = f // 4, f % 4
    spots = grads[0].reshape(2, BLOCK, 2, 64).transpose(0, 2, 1, 3).reshape(4, BLOCK, 64)
    blank = jnp.zeros_like(spots)
    odd = f % 2 == 1
    spots = jnp.concatenate([jnp.where(odd, blank, spots), jnp.where(odd, spots, blank)], axis=2)
    level0 = [0.0, 0.0]
    for r in range(4):
        pairs = [(s, ((s % 4 + r) % 4) * 4 + s // 4) for s in range(16)]
        got = send(lax.dynamic_index_in_dim(spots, (high + r) % 4, 0, False), pairs)
        second_pair = (low - r) % 4 // 2 == 1
        level0[0] = level0[0] + jnp.where(second_pair, 0.0, got)
        level0[1] = level0[1] + jnp.where(second_pair, got, 0.0)
    got = []
    for r in range(2):
        pairs = [(s, ((s % 2 + r) % 2) * 8 + s // 2) for s in range(16)]
        got.append(send(lax.dynamic_index_in_dim(grads[1], (f + r) % 2, 0, False), pairs))
    swap = f // 8 == 1
    level1 = [jnp.where(swap, got[1], got[0]), jnp.where(swap, got[0], got[1])]
    pairs = [
        (e * 16 + s, (s // 8) * 16 + 2 * (s % 8) + e) for e in range(2) for s in range(16)
    ]
    level3 = send(grads[3], pairs, ("dp", "fsdp"))
    owned = jnp.concatenate([jnp.stack(level0), jnp.stack(level1), grads[2], level3], axis=0)
    pulled = call(pull_body, shape((8, BLOCK, LANES), F32), (owned, ad))
    param_grads = (
        pulled.reshape(FACTORS, 2, BLOCK, 4, BLOCK)
        .transpose(0, 1, 3, 2, 4)
        .reshape(FACTORS, 8, BLOCK * BLOCK)
    )
    return (projected, param_grads)


def solution(mesh):
    return jax.shard_map(
        local,
        mesh=mesh,
        in_specs=(P("dp", "fsdp"), P("fsdp", "tensor"), P(), P(), P("dp", "tensor")),
        out_specs=(P(("dp", "fsdp"), "tensor"), P(None, ("dp", "fsdp"), None)),
        check_vma=False,
    )
```

```python
import functools

import jax
import jax.numpy as jnp
from jax import lax
from jax.experimental import pallas as pl
from jax.experimental.pallas import tpu as pltpu
from jax.sharding import PartitionSpec as P

BLOCK = 32
FACTORS = 4
RUN = 16
LANES = 128
BF = jnp.bfloat16
F32 = jnp.float32
HI = lax.Precision.HIGHEST


def iota(shape, dim):
    return lax.broadcasted_iota(jnp.int32, shape, dim)


def dot(a, b, ca, cb, precision=None):
    return lax.dot_general(
        a, b, (((ca,), (cb,)), ((), ())), precision=precision, preferred_element_type=F32
    )


def call(body, out_shape, args, scratch=(), limit=12 << 20):
    return pl.pallas_call(
        body,
        out_shape=out_shape,
        in_specs=[pl.BlockSpec(memory_space=pltpu.VMEM)] * len(args),
        out_specs=jax.tree.map(lambda _: pl.BlockSpec(memory_space=pltpu.VMEM), out_shape),
        scratch_shapes=list(scratch),
        compiler_params=pltpu.CompilerParams(vmem_limit_bytes=limit),
    )(*args)


def shape(dims, dtype):
    return jax.ShapeDtypeStruct(dims, dtype)


def far(x):
    return pltpu.with_memory_space_constraint(x, pltpu.HBM)


def prepare_body(
    params, perms, rot_ref, inv_ref, idx_ref, fetched, chosen, turned, mat, rows, perm_ref, sem, perm_sem
):
    f = lax.axis_index("fsdp")
    d = lax.axis_index("dp")
    copies = []

    def pull(level, start, count, to):
        source = params.at[level, pl.ds(pl.multiple_of(start, 8), count)]
        copies.append(pltpu.make_async_copy(source, fetched.at[pl.ds(to, count)], sem))

    for h in range(8):
        pull(0, h * 32 + f // 4 * 8, 8, h * 8)
    for g in range(4):
        pull(1, g * 64 + f // 2 * 8, 8, 64 + g * 8)
    for g in range(2):
        pull(2, g * 128 + f * 8, 8, 96 + g * 8)
    pull(3, f * 16, 16, 112)
    for level in range(FACTORS):
        pull(level, (d * 16 + f) * 8, 8, 128 + level * 8)
    for copy in copies:
        copy.start()
    perm_copy = pltpu.make_async_copy(perms, perm_ref, perm_sem)
    perm_copy.start()
    perm_copy.wait()

    lane = iota((1, LANES), 1)
    odd = f % 2 == 1
    half = f // 2 * LANES

    def window(level, start):
        return perm_ref[level : level + 1, pl.ds(pl.multiple_of(start, LANES), LANES)]

    for level in range(FACTORS):
        for g in range(4):
            if level == 0:
                left = window(0, 2 * g * 1024 + half)
                right = window(0, (2 * g + 1) * 1024 + half)
                left = jnp.where(odd, pltpu.roll(left, 64, 1), left)
                right = jnp.where(odd, right, pltpu.roll(right, 64, 1))
                value = jnp.where(lane < 64, left, right)
            elif level == 1:
                value = window(1, g * 2048 + f * 128)
            elif level == 2:
                value = window(2, g // 2 * 4096 + f * 256 + g % 2 * LANES)
            else:
                value = window(3, f * 512 + g * LANES)
            sigma = (value >> (9 + level) & 1) * RUN + (value & (RUN - 1))
            idx_ref[level * 4 + g : level * 4 + g + 1, :] = sigma + lane // BLOCK * BLOCK

    for copy in copies:
        copy.wait()
    for h in range(8):
        rows8 = fetched[h * 8 : h * 8 + 8, :]
        pair = rows8[:2]
        for s in range(1, 4):
            pair = jnp.where(f % 4 == s, rows8[2 * s : 2 * s + 2], pair)
        chosen[2 * h : 2 * h + 2, :] = pair
    for g in range(4):
        rows8 = fetched[64 + g * 8 : 72 + g * 8, :]
        chosen[16 + 4 * g : 20 + 4 * g, :] = jnp.where(odd, rows8[4:], rows8[:4])
    chosen[32:96, :] = fetched[96:160, :]
    chosen[96:, :] = fetched[:32, :]
    turned[...] = chosen[...].T
    sub = iota((BLOCK, LANES), 0)
    for i in range(BLOCK):
        skew = turned[i * BLOCK : (i + 1) * BLOCK, :] - turned[pl.ds(i, BLOCK, stride=BLOCK), :]
        mat[i] = jnp.where(sub == i, 1.0, 0.0) - skew

    def step(k, carry):
        here = sub == k
        pivot = 1.0 / mat[k, pl.ds(k, 1), :]
        line = jnp.where(here, pivot, mat[k] * pivot)
        for i in range(BLOCK):
            factor = mat[i, pl.ds(k, 1), :]
            mat[i] = jnp.where(here, 0.0, mat[i]) - factor * line
        mat[k] = line
        return carry

    lax.fori_loop(0, BLOCK, step, 0)
    for i in range(BLOCK):
        rows[pl.ds(i, LANES, stride=BLOCK), :] = mat[i].T
    same = iota((LANES, LANES), 0) // BLOCK == iota((LANES, LANES), 1) // BLOCK
    unit = jnp.where(iota((LANES, LANES), 0) == iota((LANES, LANES), 1), 1.0, 0.0)
    for g in range(24):
        piece = rows[g * LANES : (g + 1) * LANES, :]
        wide = jnp.where(same, jnp.concatenate([piece] * 4, axis=1), 0.0)
        if g < 16:
            rotation = (2.0 * wide - unit).astype(BF)
            rot_ref[g * LANES : (g + 1) * LANES, :] = dot(onehot(idx_ref, g), rotation, 1, 0).astype(BF)
        else:
            inv_ref[(g - 16) * LANES : (g - 15) * LANES, :] = wide


def onehot(idx_ref, g):
    return jnp.where(iota((LANES, LANES), 0) == idx_ref[g : g + 1, :], 1.0, 0.0).astype(BF)


def shuffle(x, level):
    groups = 16 >> level
    width = 512 // groups
    pieces = []
    for h in range(groups // 2):
        for i in range(width // RUN):
            for half in range(2):
                start = (2 * h + half) * width + i * RUN
                pieces.append(x[start : start + RUN])
    return jnp.concatenate(pieces, axis=0)


def unshuffle(x, level):
    groups = 16 >> level
    width = 512 // groups
    count = width // RUN
    pieces = []
    for a in range(groups):
        for i in range(count):
            start = ((a // 2) * count + i) * BLOCK + (a % 2) * RUN
            pieces.append(x[start : start + RUN])
    return jnp.concatenate(pieces, axis=0)


def forward_body(
    x_ref, rot_ref, weight, cotan, *rest, tiles
):
    parts, up_ref, saved_ref = rest[:4], rest[4], rest[5]
    w_ref, c_ref, out_ref, staged, w_sems, c_sem, p_sem = rest[6:]
    tile = weight.shape[1] // tiles
    fetches = []
    for i in range(tiles):
        span = pl.ds(i * tile, tile)
        fetches.append(pltpu.make_async_copy(weight.at[:, span], w_ref.at[:, span], w_sems.at[i]))
    fetches.append(pltpu.make_async_copy(cotan, c_ref, c_sem))
    for fetch in fetches:
        fetch.start()

    f = lax.axis_index("fsdp")
    z, x_own = f // 4, f % 4
    second = lax.axis_index("tensor") % 2 == 1
    x = x_ref[...]
    for level in range(FACTORS):
        x = shuffle(x, level)
        saved_ref[level] = x
        outs = []
        for g in range(4):
            rot = rot_ref[(level * 4 + g) * LANES : (level * 4 + g + 1) * LANES, :]
            mine = x[g * LANES : (g + 1) * LANES]
            if level < FACTORS - 1:
                outs.append(dot(rot, mine, 0, 0).astype(BF))
            else:
                outs.append(dot(mine, rot, 0, 0).astype(BF))
        x = jnp.concatenate(outs, axis=0 if level < FACTORS - 1 else 1)
    for block in range(16):
        dz, dx = (block // 4 - z + 4) % 4, (block % 4 - x_own + 4) % 4
        slot = jnp.where(second, dx * 4 + dz, dz * 4 + dx)
        out_ref[pl.ds(pl.multiple_of(slot * RUN, RUN), RUN), :] = x[block * RUN : (block + 1) * RUN]

    copies = []
    for i in range(tiles):
        span = pl.ds(i * tile, tile)
        fetches[i].wait()
        staged[i] = dot(out_ref[...], w_ref[:, span], 1, 0).astype(BF)
        for s in range(4):
            copy = pltpu.make_async_copy(staged.at[i, pl.ds(s * 64, 64)], parts[s].at[:, span], p_sem)
            copy.start()
            copies.append(copy)
    fetches[tiles].wait()
    up_ref[...] = dot(w_ref[...], c_ref[...], 1, 1).astype(BF)
    for copy in copies:
        copy.wait()


def forward(mixed, rot, weight, cotangent, tiles=7):
    depth, tokens = mixed.shape
    columns = weight.shape[1]
    vmem = pl.BlockSpec(memory_space=pltpu.VMEM)
    hbm = pl.BlockSpec(memory_space=pltpu.HBM)
    return pl.pallas_call(
        functools.partial(forward_body, tiles=tiles),
        out_shape=[pltpu.HBM((tokens // 4, columns), BF)] * 4
        + [shape((depth, tokens), BF), shape((FACTORS, depth, tokens), BF)],
        in_specs=[vmem, vmem, hbm, hbm],
        out_specs=[hbm] * 4 + [vmem] * 2,
        scratch_shapes=[
            pltpu.VMEM((depth, columns), BF),
            pltpu.VMEM((tokens, columns), BF),
            pltpu.VMEM((tokens, depth), BF),
            pltpu.VMEM((tiles, tokens, columns // tiles), BF),
            pltpu.SemaphoreType.DMA((tiles,)),
            pltpu.SemaphoreType.DMA,
            pltpu.SemaphoreType.DMA,
        ],
        compiler_params=pltpu.CompilerParams(vmem_limit_bytes=32 << 20),
    )(mixed, rot, far(weight), far(cotangent))


def backward_body(up_ref, saved_ref, rot_ref, idx_ref, grad_ref):
    d = lax.axis_index("dp")
    up = up_ref[...]
    same = iota((LANES, LANES), 0) // BLOCK == iota((LANES, LANES), 1) // BLOCK
    for level in reversed(range(FACTORS)):
        outs = []
        for g in range(4):
            base = (level * 4 + g) * LANES
            mine = up[g * LANES : (g + 1) * LANES]
            x = saved_ref[level, g * LANES : (g + 1) * LANES, :]
            moved = dot(onehot(idx_ref, level * 4 + g), x, 0, 0).astype(BF)
            outer = jnp.where(same, dot(moved, mine, 1, 1), 0.0)
            packed = outer[:BLOCK] + outer[BLOCK : 2 * BLOCK]
            packed = packed + outer[2 * BLOCK : 3 * BLOCK] + outer[3 * BLOCK :]
            grad_ref[(g // 2 + d) % 2, level, g % 2] = packed
            if level > 0:
                outs.append(dot(rot_ref[base : base + LANES, :], mine, 1, 0).astype(BF))
        if level > 0:
            up = unshuffle(jnp.concatenate(outs, axis=0), level)


def pull_body(g_ref, ad_ref, out_ref):
    same = iota((LANES, LANES), 0) // BLOCK == iota((LANES, LANES), 1) // BLOCK
    for g in range(8):
        grad = jnp.where(same, jnp.concatenate([g_ref[g]] * 4, axis=0), 0.0)
        inv = ad_ref[g * LANES : (g + 1) * LANES, :]
        both = 2.0 * dot(dot(inv, grad, 0, 0, HI), inv, 1, 1, HI)
        both = both - both.T
        packed = both[:BLOCK] + both[BLOCK : 2 * BLOCK]
        out_ref[g] = packed + both[2 * BLOCK : 3 * BLOCK] + both[3 * BLOCK :]


def ring_pairs(stage, s):
    pairs = []
    for f in range(16):
        for t in range(4):
            z, x = f // 4, f % 4
            if (t % 2) ^ stage:
                x = (x + s) % 4
            else:
                z = (z + s) % 4
            pairs.append((f * 4 + t, (z * 4 + x) * 4 + t))
    return pairs


def ring(x, stage, s):
    return lax.ppermute(x, ("fsdp", "tensor"), ring_pairs(stage, s))


def local(activations, frozen_weight, cayley_params, permutations, cotangent):
    tokens = activations.shape[0]
    mixed = lax.all_to_all(
        activations.T.reshape(16, BLOCK, tokens), "fsdp", 0, 0, tiled=True
    ).reshape(512, tokens)

    rot, inv, idx = pl.pallas_call(
        prepare_body,
        out_shape=(shape((2048, LANES), BF), shape((1024, LANES), F32), shape((16, LANES), jnp.int32)),
        in_specs=[pl.BlockSpec(memory_space=pl.ANY)] * 2,
        out_specs=(pl.BlockSpec(memory_space=pltpu.VMEM),) * 3,
        scratch_shapes=[
            pltpu.VMEM((160, BLOCK * BLOCK), F32),
            pltpu.VMEM((LANES, BLOCK * BLOCK), F32),
            pltpu.VMEM((BLOCK * BLOCK, LANES), F32),
            pltpu.VMEM((BLOCK, BLOCK, LANES), F32),
            pltpu.VMEM((BLOCK * LANES, BLOCK), F32),
            pltpu.VMEM((FACTORS, 8192), jnp.int32),
            pltpu.SemaphoreType.DMA,
            pltpu.SemaphoreType.DMA,
        ],
        compiler_params=pltpu.CompilerParams(vmem_limit_bytes=12 << 20),
    )(far(cayley_params), far(permutations))

    *parts, up, saved = forward(mixed, rot, frozen_weight, cotangent)
    near, back, across = [ring(parts[s], 0, s) for s in (1, 3, 2)]

    for bit in (1, 2):
        other = lax.ppermute(up, "tensor", [(t, t ^ bit) for t in range(4)])
        up = (up.astype(F32) + other).astype(BF)
    grads = call(
        backward_body, shape((2, FACTORS, 2, BLOCK, LANES), F32), (up, saved, rot, idx)
    )
    grads = grads[0] + lax.ppermute(grads[1], "dp", [(0, 1), (1, 0)])
    grads, near, back = lax.optimization_barrier((grads, near, back))

    f = lax.axis_index("fsdp")
    level3 = lax.ppermute(
        grads[3],
        ("dp", "fsdp"),
        [(e * 16 + s, s // 8 * 16 + s % 8 * 2 + e) for e in range(2) for s in range(16)],
    )
    spots = grads[0].reshape(2, BLOCK, 2, 64).transpose(0, 2, 1, 3).reshape(4, BLOCK, 64)
    odd = f % 2 == 1
    spots = jnp.concatenate([jnp.where(odd, 0.0, spots), jnp.where(odd, spots, 0.0)], axis=2)
    slots = jnp.stack([jnp.repeat(spots, 4, axis=0), jnp.repeat(grads[1], 8, axis=0)], axis=1)
    slots = lax.all_to_all(slots.astype(BF), "fsdp", 0, 0, tiled=True)

    across, level3 = lax.optimization_barrier((across, level3))
    parts = [parts[0], near, back, across]
    wide = [sum(p[k * RUN : (k + 1) * RUN].astype(F32) for p in parts).astype(BF) for k in range(4)]
    last = [ring(wide[s], 1, s) for s in (2, 1, 3)]

    level0 = lax.dynamic_slice_in_dim(slots[:, 0], f % 4 * 4, 4, 0).astype(F32)
    level0 = level0.reshape(2, 2, BLOCK, LANES).sum(1)
    level1 = lax.dynamic_slice_in_dim(slots[:, 1], f % 8 * 2, 2, 0).astype(F32)
    owned = jnp.concatenate([level0, level1, grads[2], level3], axis=0)
    pulled = call(pull_body, shape((8, BLOCK, LANES), F32), (owned, inv))
    param_grads = (
        pulled.reshape(FACTORS, 2, BLOCK, 4, BLOCK)
        .transpose(0, 1, 3, 2, 4)
        .reshape(FACTORS, 8, BLOCK * BLOCK)
    )
    param_grads, last = lax.optimization_barrier((param_grads, last))
    projected = sum(p.astype(F32) for p in [wide[0]] + last).astype(BF)
    return (projected, param_grads)


def solution(mesh):
    return jax.shard_map(
        local,
        mesh=mesh,
        in_specs=(P("dp", "fsdp"), P("fsdp", "tensor"), P(), P(), P("dp", "tensor")),
        out_specs=(P(("dp", "fsdp"), "tensor"), P(None, ("dp", "fsdp"), None)),
        check_vma=False,
    )
```

```python
import functools

import jax
import jax.numpy as jnp
from jax import lax
from jax.experimental import pallas as pl
from jax.experimental.pallas import tpu as pltpu
from jax.sharding import PartitionSpec as P

BLOCK = 32
FACTORS = 4
RUN = 16
LANES = 128
BF = jnp.bfloat16
F32 = jnp.float32
HI = lax.Precision.HIGHEST


def iota(shape, dim):
    return lax.broadcasted_iota(jnp.int32, shape, dim)


def dot(a, b, ca, cb, precision=None):
    return lax.dot_general(
        a, b, (((ca,), (cb,)), ((), ())), precision=precision, preferred_element_type=F32
    )


def call(body, out_shape, args, scratch=(), limit=12 << 20):
    return pl.pallas_call(
        body,
        out_shape=out_shape,
        in_specs=[pl.BlockSpec(memory_space=pltpu.VMEM)] * len(args),
        out_specs=jax.tree.map(lambda _: pl.BlockSpec(memory_space=pltpu.VMEM), out_shape),
        scratch_shapes=list(scratch),
        compiler_params=pltpu.CompilerParams(vmem_limit_bytes=limit),
    )(*args)


def shape(dims, dtype):
    return jax.ShapeDtypeStruct(dims, dtype)


def far(x):
    return pltpu.with_memory_space_constraint(x, pltpu.HBM)


def prepare_body(
    params,
    perms,
    weight,
    cotan,
    rot_ref,
    inv_ref,
    idx_ref,
    up_ref,
    w_ref,
    c_ref,
    fetched,
    chosen,
    turned,
    mat,
    rows,
    perm_ref,
    sem,
    perm_sem,
    w_sem,
    c_sem,
):
    f = lax.axis_index("fsdp")
    d = lax.axis_index("dp")
    copies = []

    def pull(level, start, count, to):
        source = params.at[level, pl.ds(pl.multiple_of(start, 8), count)]
        copies.append(pltpu.make_async_copy(source, fetched.at[pl.ds(to, count)], sem))

    for h in range(8):
        pull(0, h * 32 + f // 4 * 8, 8, h * 8)
    for g in range(4):
        pull(1, g * 64 + f // 2 * 8, 8, 64 + g * 8)
    for g in range(2):
        pull(2, g * 128 + f * 8, 8, 96 + g * 8)
    pull(3, f * 16, 16, 112)
    for level in range(FACTORS):
        pull(level, (d * 16 + f) * 8, 8, 128 + level * 8)
    for copy in copies:
        copy.start()
    perm_copy = pltpu.make_async_copy(perms, perm_ref, perm_sem)
    perm_copy.start()
    w_copy = pltpu.make_async_copy(weight, w_ref, w_sem)
    w_copy.start()
    c_copy = pltpu.make_async_copy(cotan, c_ref, c_sem)
    c_copy.start()
    perm_copy.wait()

    lane = iota((1, LANES), 1)
    odd = f % 2 == 1
    half = f // 2 * LANES

    def window(level, start):
        return perm_ref[level : level + 1, pl.ds(pl.multiple_of(start, LANES), LANES)]

    for level in range(FACTORS):
        for g in range(4):
            if level == 0:
                left = window(0, 2 * g * 1024 + half)
                right = window(0, (2 * g + 1) * 1024 + half)
                left = jnp.where(odd, pltpu.roll(left, 64, 1), left)
                right = jnp.where(odd, right, pltpu.roll(right, 64, 1))
                value = jnp.where(lane < 64, left, right)
            elif level == 1:
                value = window(1, g * 2048 + f * 128)
            elif level == 2:
                value = window(2, g // 2 * 4096 + f * 256 + g % 2 * LANES)
            else:
                value = window(3, f * 512 + g * LANES)
            sigma = (value >> (9 + level) & 1) * RUN + (value & (RUN - 1))
            idx_ref[level * 4 + g : level * 4 + g + 1, :] = sigma + lane // BLOCK * BLOCK

    for copy in copies:
        copy.wait()
    for h in range(8):
        rows8 = fetched[h * 8 : h * 8 + 8, :]
        pair = rows8[:2]
        for s in range(1, 4):
            pair = jnp.where(f % 4 == s, rows8[2 * s : 2 * s + 2], pair)
        chosen[2 * h : 2 * h + 2, :] = pair
    for g in range(4):
        rows8 = fetched[64 + g * 8 : 72 + g * 8, :]
        chosen[16 + 4 * g : 20 + 4 * g, :] = jnp.where(odd, rows8[4:], rows8[:4])
    chosen[32:96, :] = fetched[96:160, :]
    chosen[96:, :] = fetched[:32, :]
    turned[...] = chosen[...].T
    sub = iota((BLOCK, LANES), 0)
    for i in range(BLOCK):
        skew = turned[i * BLOCK : (i + 1) * BLOCK, :] - turned[pl.ds(i, BLOCK, stride=BLOCK), :]
        mat[i] = jnp.where(sub == i, 1.0, 0.0) - skew

    def step(k, carry):
        here = sub == k
        pivot = 1.0 / mat[k, pl.ds(k, 1), :]
        line = jnp.where(here, pivot, mat[k] * pivot)
        for i in range(BLOCK):
            factor = mat[i, pl.ds(k, 1), :]
            mat[i] = jnp.where(here, 0.0, mat[i]) - factor * line
        mat[k] = line
        return carry

    lax.fori_loop(0, BLOCK, step, 0)
    for i in range(BLOCK):
        rows[pl.ds(i, LANES, stride=BLOCK), :] = mat[i].T
    same = iota((LANES, LANES), 0) // BLOCK == iota((LANES, LANES), 1) // BLOCK
    unit = jnp.where(iota((LANES, LANES), 0) == iota((LANES, LANES), 1), 1.0, 0.0)
    for g in range(24):
        piece = rows[g * LANES : (g + 1) * LANES, :]
        wide = jnp.where(same, jnp.concatenate([piece] * 4, axis=1), 0.0)
        if g < 16:
            rotation = (2.0 * wide - unit).astype(BF)
            rot_ref[g * LANES : (g + 1) * LANES, :] = dot(onehot(idx_ref, g), rotation, 1, 0).astype(BF)
        else:
            inv_ref[(g - 16) * LANES : (g - 15) * LANES, :] = wide
    w_copy.wait()
    c_copy.wait()
    up_ref[...] = dot(w_ref[...], c_ref[...], 1, 1).astype(BF)


def onehot(idx_ref, g):
    return jnp.where(iota((LANES, LANES), 0) == idx_ref[g : g + 1, :], 1.0, 0.0).astype(BF)


def shuffle(x, level):
    groups = 16 >> level
    width = 512 // groups
    pieces = []
    for h in range(groups // 2):
        for i in range(width // RUN):
            for half in range(2):
                start = (2 * h + half) * width + i * RUN
                pieces.append(x[start : start + RUN])
    return jnp.concatenate(pieces, axis=0)


def unshuffle(x, level):
    groups = 16 >> level
    width = 512 // groups
    count = width // RUN
    pieces = []
    for a in range(groups):
        for i in range(count):
            start = ((a // 2) * count + i) * BLOCK + (a % 2) * RUN
            pieces.append(x[start : start + RUN])
    return jnp.concatenate(pieces, axis=0)


def forward_body(
    x_ref, rot_ref, weight, *rest, tiles
):
    parts, saved_ref = rest[:4], rest[4]
    w_ref, out_ref, staged, w_sems, p_sem = rest[5:]
    tile = weight.shape[1] // tiles
    fetches = []
    for i in range(tiles):
        span = pl.ds(i * tile, tile)
        fetches.append(pltpu.make_async_copy(weight.at[:, span], w_ref.at[:, span], w_sems.at[i]))
    for fetch in fetches:
        fetch.start()

    f = lax.axis_index("fsdp")
    z, x_own = f // 4, f % 4
    second = lax.axis_index("tensor") % 2 == 1
    x = x_ref[...]
    for level in range(FACTORS):
        x = shuffle(x, level)
        saved_ref[level] = x
        outs = []
        for g in range(4):
            rot = rot_ref[(level * 4 + g) * LANES : (level * 4 + g + 1) * LANES, :]
            mine = x[g * LANES : (g + 1) * LANES]
            if level < FACTORS - 1:
                outs.append(dot(rot, mine, 0, 0).astype(BF))
            else:
                outs.append(dot(mine, rot, 0, 0).astype(BF))
        x = jnp.concatenate(outs, axis=0 if level < FACTORS - 1 else 1)
    for block in range(16):
        dz, dx = (block // 4 - z + 4) % 4, (block % 4 - x_own + 4) % 4
        slot = jnp.where(second, dx * 4 + dz, dz * 4 + dx)
        out_ref[pl.ds(pl.multiple_of(slot * RUN, RUN), RUN), :] = x[block * RUN : (block + 1) * RUN]

    copies = []
    for i in range(tiles):
        span = pl.ds(i * tile, tile)
        fetches[i].wait()
        staged[i] = dot(out_ref[...], w_ref[:, span], 1, 0).astype(BF)
        for s in range(4):
            copy = pltpu.make_async_copy(staged.at[i, pl.ds(s * 64, 64)], parts[s].at[:, span], p_sem)
            copy.start()
            copies.append(copy)
    for copy in copies:
        copy.wait()


def forward(mixed, rot, weight, tiles=7):
    depth, tokens = mixed.shape
    columns = weight.shape[1]
    vmem = pl.BlockSpec(memory_space=pltpu.VMEM)
    hbm = pl.BlockSpec(memory_space=pltpu.HBM)
    return pl.pallas_call(
        functools.partial(forward_body, tiles=tiles),
        out_shape=[pltpu.HBM((tokens // 4, columns), BF)] * 4
        + [shape((FACTORS, depth, tokens), BF)],
        in_specs=[vmem, vmem, hbm],
        out_specs=[hbm] * 4 + [vmem],
        scratch_shapes=[
            pltpu.VMEM((depth, columns), BF),
            pltpu.VMEM((tokens, depth), BF),
            pltpu.VMEM((tiles, tokens, columns // tiles), BF),
            pltpu.SemaphoreType.DMA((tiles,)),
            pltpu.SemaphoreType.DMA,
        ],
        compiler_params=pltpu.CompilerParams(vmem_limit_bytes=32 << 20),
    )(mixed, rot, far(weight))


def backward_body(up_ref, saved_ref, rot_ref, idx_ref, grad_ref):
    d = lax.axis_index("dp")
    up = up_ref[...]
    same = iota((LANES, LANES), 0) // BLOCK == iota((LANES, LANES), 1) // BLOCK
    for level in reversed(range(FACTORS)):
        outs = []
        for g in range(4):
            base = (level * 4 + g) * LANES
            mine = up[g * LANES : (g + 1) * LANES]
            x = saved_ref[level, g * LANES : (g + 1) * LANES, :]
            moved = dot(onehot(idx_ref, level * 4 + g), x, 0, 0).astype(BF)
            outer = jnp.where(same, dot(moved, mine, 1, 1), 0.0)
            packed = outer[:BLOCK] + outer[BLOCK : 2 * BLOCK]
            packed = packed + outer[2 * BLOCK : 3 * BLOCK] + outer[3 * BLOCK :]
            grad_ref[(g // 2 + d) % 2, level, g % 2] = packed
            if level > 0:
                outs.append(dot(rot_ref[base : base + LANES, :], mine, 1, 0).astype(BF))
        if level > 0:
            up = unshuffle(jnp.concatenate(outs, axis=0), level)


def pull_body(g_ref, ad_ref, out_ref):
    same = iota((LANES, LANES), 0) // BLOCK == iota((LANES, LANES), 1) // BLOCK
    for g in range(8):
        grad = jnp.where(same, jnp.concatenate([g_ref[g]] * 4, axis=0), 0.0)
        inv = ad_ref[g * LANES : (g + 1) * LANES, :]
        both = 2.0 * dot(dot(inv, grad, 0, 0, HI), inv, 1, 1, HI)
        both = both - both.T
        packed = both[:BLOCK] + both[BLOCK : 2 * BLOCK]
        out_ref[g] = packed + both[2 * BLOCK : 3 * BLOCK] + both[3 * BLOCK :]


def ring_pairs(stage, s):
    pairs = []
    for f in range(16):
        for t in range(4):
            z, x = f // 4, f % 4
            if (t % 2) ^ stage:
                x = (x + s) % 4
            else:
                z = (z + s) % 4
            pairs.append((f * 4 + t, (z * 4 + x) * 4 + t))
    return pairs


def ring(x, stage, s):
    return lax.ppermute(x, ("fsdp", "tensor"), ring_pairs(stage, s))


def local(activations, frozen_weight, cayley_params, permutations, cotangent):
    tokens = activations.shape[0]
    mixed = lax.all_to_all(
        activations.T.reshape(16, BLOCK, tokens), "fsdp", 0, 0, tiled=True
    ).reshape(512, tokens)

    rot, inv, idx, up = pl.pallas_call(
        prepare_body,
        out_shape=(
            shape((2048, LANES), BF),
            shape((1024, LANES), F32),
            shape((16, LANES), jnp.int32),
            shape((512, tokens), BF),
        ),
        in_specs=[pl.BlockSpec(memory_space=pltpu.HBM)] * 4,
        out_specs=(pl.BlockSpec(memory_space=pltpu.VMEM),) * 4,
        scratch_shapes=[
            pltpu.VMEM(frozen_weight.shape, BF),
            pltpu.VMEM(cotangent.shape, BF),
            pltpu.VMEM((160, BLOCK * BLOCK), F32),
            pltpu.VMEM((LANES, BLOCK * BLOCK), F32),
            pltpu.VMEM((BLOCK * BLOCK, LANES), F32),
            pltpu.VMEM((BLOCK, BLOCK, LANES), F32),
            pltpu.VMEM((BLOCK * LANES, BLOCK), F32),
            pltpu.VMEM((FACTORS, 8192), jnp.int32),
            pltpu.SemaphoreType.DMA,
            pltpu.SemaphoreType.DMA,
            pltpu.SemaphoreType.DMA,
            pltpu.SemaphoreType.DMA,
        ],
        compiler_params=pltpu.CompilerParams(vmem_limit_bytes=32 << 20),
    )(far(cayley_params), far(permutations), far(frozen_weight), far(cotangent))

    up, mixed = lax.optimization_barrier((up, mixed))
    *parts, saved = forward(mixed, rot, frozen_weight)
    near, back, across = [ring(parts[s], 0, s) for s in (1, 3, 2)]

    for bit in (1, 2):
        other = lax.ppermute(up, "tensor", [(t, t ^ bit) for t in range(4)])
        up = (up.astype(F32) + other).astype(BF)
    grads = call(
        backward_body, shape((2, FACTORS, 2, BLOCK, LANES), F32), (up, saved, rot, idx)
    )
    grads = grads[0] + lax.ppermute(grads[1], "dp", [(0, 1), (1, 0)])
    grads, near = lax.optimization_barrier((grads, near))

    f = lax.axis_index("fsdp")
    level3 = lax.ppermute(
        grads[3],
        ("dp", "fsdp"),
        [(e * 16 + s, s // 8 * 16 + s % 8 * 2 + e) for e in range(2) for s in range(16)],
    )
    spots = grads[0].reshape(2, BLOCK, 2, 64).transpose(0, 2, 1, 3).reshape(4, BLOCK, 64)
    odd = f % 2 == 1
    spots = jnp.concatenate([jnp.where(odd, 0.0, spots), jnp.where(odd, spots, 0.0)], axis=2)
    slots = jnp.stack([jnp.repeat(spots, 4, axis=0), jnp.repeat(grads[1], 8, axis=0)], axis=1)
    slots = lax.all_to_all(slots.astype(BF), "fsdp", 0, 0, tiled=True)

    across, level3 = lax.optimization_barrier((across, level3))
    parts = [parts[0], near, back, across]
    wide = [sum(p[k * RUN : (k + 1) * RUN].astype(F32) for p in parts).astype(BF) for k in range(4)]
    last = [ring(wide[s], 1, s) for s in (2, 1, 3)]

    level0 = lax.dynamic_slice_in_dim(slots[:, 0], f % 4 * 4, 4, 0).astype(F32)
    level0 = level0.reshape(2, 2, BLOCK, LANES).sum(1)
    level1 = lax.dynamic_slice_in_dim(slots[:, 1], f % 8 * 2, 2, 0).astype(F32)
    owned = jnp.concatenate([level0, level1, grads[2], level3], axis=0)
    pulled = call(pull_body, shape((8, BLOCK, LANES), F32), (owned, inv))
    param_grads = (
        pulled.reshape(FACTORS, 2, BLOCK, 4, BLOCK)
        .transpose(0, 1, 3, 2, 4)
        .reshape(FACTORS, 8, BLOCK * BLOCK)
    )
    param_grads, last = lax.optimization_barrier((param_grads, last))
    projected = sum(p.astype(F32) for p in [wide[0]] + last).astype(BF)
    return (projected, param_grads)


def solution(mesh):
    return jax.shard_map(
        local,
        mesh=mesh,
        in_specs=(P("dp", "fsdp"), P("fsdp", "tensor"), P(), P(), P("dp", "tensor")),
        out_specs=(P(("dp", "fsdp"), "tensor"), P(None, ("dp", "fsdp"), None)),
        check_vma=False,
    )
```

```python
import functools

import jax
import jax.numpy as jnp
from jax import lax
from jax.experimental import pallas as pl
from jax.experimental.pallas import tpu as pltpu
from jax.sharding import PartitionSpec as P

BLOCK = 32
FACTORS = 4
RUN = 16
LANES = 128
BF = jnp.bfloat16
F32 = jnp.float32
HI = lax.Precision.HIGHEST


def iota(shape, dim):
    return lax.broadcasted_iota(jnp.int32, shape, dim)


def dot(a, b, ca, cb, precision=None):
    return lax.dot_general(
        a, b, (((ca,), (cb,)), ((), ())), precision=precision, preferred_element_type=F32
    )


def call(body, out_shape, args, scratch=(), limit=12 << 20):
    return pl.pallas_call(
        body,
        out_shape=out_shape,
        in_specs=[pl.BlockSpec(memory_space=pltpu.VMEM)] * len(args),
        out_specs=jax.tree.map(lambda _: pl.BlockSpec(memory_space=pltpu.VMEM), out_shape),
        scratch_shapes=list(scratch),
        compiler_params=pltpu.CompilerParams(vmem_limit_bytes=limit),
    )(*args)


def shape(dims, dtype):
    return jax.ShapeDtypeStruct(dims, dtype)


def far(x):
    return pltpu.with_memory_space_constraint(x, pltpu.HBM)


def prepare_body(
    params,
    perms,
    weight,
    cotan,
    rot_ref,
    inv_ref,
    idx_ref,
    up_ref,
    w_ref,
    c_ref,
    fetched,
    chosen,
    turned,
    mat,
    rows,
    perm_ref,
    sem,
    perm_sem,
    w_sem,
    c_sem,
):
    f = lax.axis_index("fsdp")
    d = lax.axis_index("dp")
    copies = []

    def pull(level, start, count, to):
        source = params.at[level, pl.ds(pl.multiple_of(start, 8), count)]
        copies.append(pltpu.make_async_copy(source, fetched.at[pl.ds(to, count)], sem))

    for h in range(8):
        pull(0, h * 32 + f // 4 * 8, 8, h * 8)
    for g in range(4):
        pull(1, g * 64 + f // 2 * 8, 8, 64 + g * 8)
    for g in range(2):
        pull(2, g * 128 + f * 8, 8, 96 + g * 8)
    pull(3, f * 16, 16, 112)
    for level in range(FACTORS):
        pull(level, (d * 16 + f) * 8, 8, 128 + level * 8)
    for copy in copies:
        copy.start()
    perm_copy = pltpu.make_async_copy(perms, perm_ref, perm_sem)
    perm_copy.start()
    w_copy = pltpu.make_async_copy(weight, w_ref, w_sem)
    w_copy.start()
    c_copy = pltpu.make_async_copy(cotan, c_ref, c_sem)
    c_copy.start()
    perm_copy.wait()

    lane = iota((1, LANES), 1)
    odd = f % 2 == 1
    half = f // 2 * LANES

    def window(level, start):
        return perm_ref[level : level + 1, pl.ds(pl.multiple_of(start, LANES), LANES)]

    for level in range(FACTORS):
        for g in range(4):
            if level == 0:
                left = window(0, 2 * g * 1024 + half)
                right = window(0, (2 * g + 1) * 1024 + half)
                left = jnp.where(odd, pltpu.roll(left, 64, 1), left)
                right = jnp.where(odd, right, pltpu.roll(right, 64, 1))
                value = jnp.where(lane < 64, left, right)
            elif level == 1:
                value = window(1, g * 2048 + f * 128)
            elif level == 2:
                value = window(2, g // 2 * 4096 + f * 256 + g % 2 * LANES)
            else:
                value = window(3, f * 512 + g * LANES)
            sigma = (value >> (9 + level) & 1) * RUN + (value & (RUN - 1))
            idx_ref[level * 4 + g : level * 4 + g + 1, :] = sigma + lane // BLOCK * BLOCK

    for copy in copies:
        copy.wait()
    for h in range(8):
        rows8 = fetched[h * 8 : h * 8 + 8, :]
        pair = rows8[:2]
        for s in range(1, 4):
            pair = jnp.where(f % 4 == s, rows8[2 * s : 2 * s + 2], pair)
        chosen[2 * h : 2 * h + 2, :] = pair
    for g in range(4):
        rows8 = fetched[64 + g * 8 : 72 + g * 8, :]
        chosen[16 + 4 * g : 20 + 4 * g, :] = jnp.where(odd, rows8[4:], rows8[:4])
    chosen[32:96, :] = fetched[96:160, :]
    chosen[96:, :] = fetched[:32, :]
    turned[...] = chosen[...].T
    sub = iota((BLOCK, LANES), 0)
    for i in range(BLOCK):
        skew = turned[i * BLOCK : (i + 1) * BLOCK, :] - turned[pl.ds(i, BLOCK, stride=BLOCK), :]
        mat[i] = jnp.where(sub == i, 1.0, 0.0) - skew

    def step(pair, carry):
        k = 2 * pair
        here, next_here = sub == k, sub == k + 1
        either = here | next_here
        pivot = 1.0 / mat[k, pl.ds(k, 1), :]
        first = jnp.where(here, pivot, mat[k] * pivot)
        first_next = mat[k, pl.ds(k + 1, 1), :] * pivot
        factor = mat[k + 1, pl.ds(k, 1), :]
        second = jnp.where(here, 0.0, mat[k + 1]) - factor * first
        pivot = 1.0 / (mat[k + 1, pl.ds(k + 1, 1), :] - factor * first_next)
        second = jnp.where(next_here, pivot, second * pivot)
        cut = jnp.where(next_here, 0.0, first)
        for i in range(BLOCK):
            factor = mat[i, pl.ds(k, 1), :]
            after = mat[i, pl.ds(k + 1, 1), :] - factor * first_next
            mat[i] = jnp.where(either, 0.0, mat[i]) - factor * cut - after * second
        mat[k] = cut - first_next * second
        mat[k + 1] = second
        return carry

    lax.fori_loop(0, BLOCK // 2, step, 0)
    for i in range(BLOCK):
        rows[pl.ds(i, 96, stride=BLOCK), :] = mat[i].T[:96]
    same = iota((LANES, LANES), 0) // BLOCK == iota((LANES, LANES), 1) // BLOCK
    spread = jnp.where(iota((BLOCK, LANES), 0) == iota((BLOCK, LANES), 1) % BLOCK, 1.0, 0.0).astype(BF)
    unit = jnp.where(iota((LANES, BLOCK), 0) % BLOCK == iota((LANES, BLOCK), 1), 1.0, 0.0)
    for g in range(24):
        piece = rows[g * LANES : (g + 1) * LANES, :]
        if g < 16:
            rotation = dot((2.0 * piece - unit).astype(BF), spread, 1, 0)
            rotation = jnp.where(same, rotation, 0.0).astype(BF)
            rot_ref[g * LANES : (g + 1) * LANES, :] = dot(onehot(idx_ref, g), rotation, 1, 0).astype(BF)
        else:
            wide = jnp.where(same, jnp.concatenate([piece] * 4, axis=1), 0.0)
            inv_ref[(g - 16) * LANES : (g - 15) * LANES, :] = wide
    w_copy.wait()
    c_copy.wait()
    up_ref[...] = dot(w_ref[...], c_ref[...], 1, 1).astype(BF)


def onehot(idx_ref, g):
    return jnp.where(iota((LANES, LANES), 0) == idx_ref[g : g + 1, :], 1.0, 0.0).astype(BF)


def shuffle(x, level):
    groups = 16 >> level
    width = 512 // groups
    pieces = []
    for h in range(groups // 2):
        for i in range(width // RUN):
            for half in range(2):
                start = (2 * h + half) * width + i * RUN
                pieces.append(x[start : start + RUN])
    return jnp.concatenate(pieces, axis=0)


def unshuffle(x, level):
    groups = 16 >> level
    width = 512 // groups
    count = width // RUN
    pieces = []
    for a in range(groups):
        for i in range(count):
            start = ((a // 2) * count + i) * BLOCK + (a % 2) * RUN
            pieces.append(x[start : start + RUN])
    return jnp.concatenate(pieces, axis=0)


def forward_body(
    x_ref, rot_ref, weight, *rest, tiles
):
    parts, saved_ref = rest[:4], rest[4]
    w_ref, out_ref, staged, w_sems, p_sem = rest[5:]
    tile = weight.shape[1] // tiles
    fetches = []
    for i in range(tiles):
        span = pl.ds(i * tile, tile)
        fetches.append(pltpu.make_async_copy(weight.at[:, span], w_ref.at[:, span], w_sems.at[i]))
    for fetch in fetches:
        fetch.start()

    f = lax.axis_index("fsdp")
    z, x_own = f // 4, f % 4
    second = lax.axis_index("tensor") % 2 == 1
    x = x_ref[...]
    for level in range(FACTORS):
        x = shuffle(x, level)
        saved_ref[level] = x
        outs = []
        for g in range(4):
            rot = rot_ref[(level * 4 + g) * LANES : (level * 4 + g + 1) * LANES, :]
            mine = x[g * LANES : (g + 1) * LANES]
            if level < FACTORS - 1:
                outs.append(dot(rot, mine, 0, 0).astype(BF))
            else:
                outs.append(dot(mine, rot, 0, 0).astype(BF))
        x = jnp.concatenate(outs, axis=0 if level < FACTORS - 1 else 1)
    for block in range(16):
        dz, dx = (block // 4 - z + 4) % 4, (block % 4 - x_own + 4) % 4
        slot = jnp.where(second, dx * 4 + dz, dz * 4 + dx)
        out_ref[pl.ds(pl.multiple_of(slot * RUN, RUN), RUN), :] = x[block * RUN : (block + 1) * RUN]

    copies = []
    for i in range(tiles):
        span = pl.ds(i * tile, tile)
        fetches[i].wait()
        staged[i] = dot(out_ref[...], w_ref[:, span], 1, 0).astype(BF)
        for s in range(4):
            copy = pltpu.make_async_copy(staged.at[i, pl.ds(s * 64, 64)], parts[s].at[:, span], p_sem)
            copy.start()
            copies.append(copy)
    for copy in copies:
        copy.wait()


def forward(mixed, rot, weight, tiles=7):
    depth, tokens = mixed.shape
    columns = weight.shape[1]
    vmem = pl.BlockSpec(memory_space=pltpu.VMEM)
    hbm = pl.BlockSpec(memory_space=pltpu.HBM)
    return pl.pallas_call(
        functools.partial(forward_body, tiles=tiles),
        out_shape=[pltpu.HBM((tokens // 4, columns), BF)] * 4
        + [shape((FACTORS, depth, tokens), BF)],
        in_specs=[vmem, vmem, hbm],
        out_specs=[hbm] * 4 + [vmem],
        scratch_shapes=[
            pltpu.VMEM((depth, columns), BF),
            pltpu.VMEM((tokens, depth), BF),
            pltpu.VMEM((tiles, tokens, columns // tiles), BF),
            pltpu.SemaphoreType.DMA((tiles,)),
            pltpu.SemaphoreType.DMA,
        ],
        compiler_params=pltpu.CompilerParams(vmem_limit_bytes=32 << 20),
    )(mixed, rot, far(weight))


def backward_body(up_ref, saved_ref, rot_ref, idx_ref, grad_ref):
    d = lax.axis_index("dp")
    up = up_ref[...]
    same = iota((LANES, LANES), 0) // BLOCK == iota((LANES, LANES), 1) // BLOCK
    for level in reversed(range(FACTORS)):
        outs = []
        for g in range(4):
            base = (level * 4 + g) * LANES
            mine = up[g * LANES : (g + 1) * LANES]
            x = saved_ref[level, g * LANES : (g + 1) * LANES, :]
            moved = dot(onehot(idx_ref, level * 4 + g), x, 0, 0).astype(BF)
            outer = jnp.where(same, dot(moved, mine, 1, 1), 0.0)
            packed = outer[:BLOCK] + outer[BLOCK : 2 * BLOCK]
            packed = packed + outer[2 * BLOCK : 3 * BLOCK] + outer[3 * BLOCK :]
            grad_ref[(g // 2 + d) % 2, level, g % 2] = packed
            if level > 0:
                outs.append(dot(rot_ref[base : base + LANES, :], mine, 1, 0).astype(BF))
        if level > 0:
            up = unshuffle(jnp.concatenate(outs, axis=0), level)


def pull_body(g_ref, ad_ref, out_ref):
    same = iota((LANES, LANES), 0) // BLOCK == iota((LANES, LANES), 1) // BLOCK
    for g in range(8):
        grad = jnp.where(same, jnp.concatenate([g_ref[g]] * 4, axis=0), 0.0)
        inv = ad_ref[g * LANES : (g + 1) * LANES, :]
        both = 2.0 * dot(dot(inv, grad, 0, 0, HI), inv, 1, 1, HI)
        both = both - both.T
        packed = both[:BLOCK] + both[BLOCK : 2 * BLOCK]
        out_ref[g] = packed + both[2 * BLOCK : 3 * BLOCK] + both[3 * BLOCK :]


def ring_pairs(stage, s):
    pairs = []
    for f in range(16):
        for t in range(4):
            z, x = f // 4, f % 4
            if (t % 2) ^ stage:
                x = (x + s) % 4
            else:
                z = (z + s) % 4
            pairs.append((f * 4 + t, (z * 4 + x) * 4 + t))
    return pairs


def ring(x, stage, s):
    return lax.ppermute(x, ("fsdp", "tensor"), ring_pairs(stage, s))


def local(activations, frozen_weight, cayley_params, permutations, cotangent):
    tokens = activations.shape[0]
    mixed = lax.all_to_all(
        activations.T.reshape(16, BLOCK, tokens), "fsdp", 0, 0, tiled=True
    ).reshape(512, tokens)

    rot, inv, idx, up = pl.pallas_call(
        prepare_body,
        out_shape=(
            shape((2048, LANES), BF),
            shape((1024, LANES), F32),
            shape((16, LANES), jnp.int32),
            shape((512, tokens), BF),
        ),
        in_specs=[pl.BlockSpec(memory_space=pltpu.HBM)] * 4,
        out_specs=(pl.BlockSpec(memory_space=pltpu.VMEM),) * 4,
        scratch_shapes=[
            pltpu.VMEM(frozen_weight.shape, BF),
            pltpu.VMEM(cotangent.shape, BF),
            pltpu.VMEM((160, BLOCK * BLOCK), F32),
            pltpu.VMEM((LANES, BLOCK * BLOCK), F32),
            pltpu.VMEM((BLOCK * BLOCK, LANES), F32),
            pltpu.VMEM((BLOCK, BLOCK, LANES), F32),
            pltpu.VMEM((BLOCK * 96, BLOCK), F32),
            pltpu.VMEM((FACTORS, 8192), jnp.int32),
            pltpu.SemaphoreType.DMA,
            pltpu.SemaphoreType.DMA,
            pltpu.SemaphoreType.DMA,
            pltpu.SemaphoreType.DMA,
        ],
        compiler_params=pltpu.CompilerParams(vmem_limit_bytes=32 << 20),
    )(far(cayley_params), far(permutations), far(frozen_weight), far(cotangent))

    up, mixed = lax.optimization_barrier((up, mixed))
    *parts, saved = forward(mixed, rot, frozen_weight)
    near, back, across = [ring(parts[s], 0, s) for s in (1, 3, 2)]

    for bit in (1, 2):
        other = lax.ppermute(up, "tensor", [(t, t ^ bit) for t in range(4)])
        up = (up.astype(F32) + other).astype(BF)
    grads = call(
        backward_body, shape((2, FACTORS, 2, BLOCK, LANES), F32), (up, saved, rot, idx)
    )
    grads = grads[0] + lax.ppermute(grads[1], "dp", [(0, 1), (1, 0)])
    grads, near = lax.optimization_barrier((grads, near))

    f = lax.axis_index("fsdp")
    level3 = lax.ppermute(
        grads[3],
        ("dp", "fsdp"),
        [(e * 16 + s, s // 8 * 16 + s % 8 * 2 + e) for e in range(2) for s in range(16)],
    )
    spots = grads[0].reshape(2, BLOCK, 2, 64).transpose(0, 2, 1, 3).reshape(4, BLOCK, 64)
    odd = f % 2 == 1
    spots = jnp.concatenate([jnp.where(odd, 0.0, spots), jnp.where(odd, spots, 0.0)], axis=2)
    slots = jnp.stack([jnp.repeat(spots, 4, axis=0), jnp.repeat(grads[1], 8, axis=0)], axis=1)
    slots = lax.all_to_all(slots.astype(BF), "fsdp", 0, 0, tiled=True)

    across, level3 = lax.optimization_barrier((across, level3))
    parts = [parts[0], near, back, across]
    wide = [sum(p[k * RUN : (k + 1) * RUN].astype(F32) for p in parts).astype(BF) for k in range(4)]
    last = [ring(wide[s], 1, s) for s in (2, 1, 3)]

    level0 = lax.dynamic_slice_in_dim(slots[:, 0], f % 4 * 4, 4, 0).astype(F32)
    level0 = level0.reshape(2, 2, BLOCK, LANES).sum(1)
    level1 = lax.dynamic_slice_in_dim(slots[:, 1], f % 8 * 2, 2, 0).astype(F32)
    owned = jnp.concatenate([level0, level1, grads[2], level3], axis=0)
    pulled = call(pull_body, shape((8, BLOCK, LANES), F32), (owned, inv))
    param_grads = (
        pulled.reshape(FACTORS, 2, BLOCK, 4, BLOCK)
        .transpose(0, 1, 3, 2, 4)
        .reshape(FACTORS, 8, BLOCK * BLOCK)
    )
    param_grads, last = lax.optimization_barrier((param_grads, last))
    projected = sum(p.astype(F32) for p in [wide[0]] + last).astype(BF)
    return (projected, param_grads)


def solution(mesh):
    return jax.shard_map(
        local,
        mesh=mesh,
        in_specs=(P("dp", "fsdp"), P("fsdp", "tensor"), P(), P(), P("dp", "tensor")),
        out_specs=(P(("dp", "fsdp"), "tensor"), P(None, ("dp", "fsdp"), None)),
        check_vma=False,
    )
```

```python
import functools

import jax
import jax.numpy as jnp
from jax import lax
from jax.experimental import pallas as pl
from jax.experimental.pallas import tpu as pltpu
from jax.sharding import PartitionSpec as P

BLOCK = 32
FACTORS = 4
RUN = 16
LANES = 128
BF = jnp.bfloat16
F32 = jnp.float32
HI = lax.Precision.HIGHEST


def iota(shape, dim):
    return lax.broadcasted_iota(jnp.int32, shape, dim)


def dot(a, b, ca, cb, precision=None):
    return lax.dot_general(
        a, b, (((ca,), (cb,)), ((), ())), precision=precision, preferred_element_type=F32
    )


def call(body, out_shape, args, scratch=(), limit=12 << 20):
    return pl.pallas_call(
        body,
        out_shape=out_shape,
        in_specs=[pl.BlockSpec(memory_space=pltpu.VMEM)] * len(args),
        out_specs=jax.tree.map(lambda _: pl.BlockSpec(memory_space=pltpu.VMEM), out_shape),
        scratch_shapes=list(scratch),
        compiler_params=pltpu.CompilerParams(vmem_limit_bytes=limit),
    )(*args)


def shape(dims, dtype):
    return jax.ShapeDtypeStruct(dims, dtype)


def far(x):
    return pltpu.with_memory_space_constraint(x, pltpu.HBM)


def prepare_body(
    params,
    perms,
    weight,
    cotan,
    rot_ref,
    inv_ref,
    idx_ref,
    up_ref,
    w_ref,
    c_ref,
    fetched,
    chosen,
    turned,
    mat,
    rows,
    perm_ref,
    sem,
    perm_sem,
    w_sem,
    c_sem,
):
    f = lax.axis_index("fsdp")
    d = lax.axis_index("dp")
    copies = []

    def pull(level, start, count, to):
        source = params.at[level, pl.ds(pl.multiple_of(start, 8), count)]
        copies.append(pltpu.make_async_copy(source, fetched.at[pl.ds(to, count)], sem))

    for h in range(8):
        pull(0, h * 32 + f // 4 * 8, 8, h * 8)
    for g in range(4):
        pull(1, g * 64 + f // 2 * 8, 8, 64 + g * 8)
    for g in range(2):
        pull(2, g * 128 + f * 8, 8, 96 + g * 8)
    pull(3, f * 16, 16, 112)
    for level in range(FACTORS):
        pull(level, (d * 16 + f) * 8, 8, 128 + level * 8)
    for copy in copies:
        copy.start()
    perm_copy = pltpu.make_async_copy(perms, perm_ref, perm_sem)
    perm_copy.start()
    w_copy = pltpu.make_async_copy(weight, w_ref, w_sem)
    w_copy.start()
    c_copy = pltpu.make_async_copy(cotan, c_ref, c_sem)
    c_copy.start()
    perm_copy.wait()

    lane = iota((1, LANES), 1)
    odd = f % 2 == 1
    half = f // 2 * LANES

    def window(level, start):
        return perm_ref[level : level + 1, pl.ds(pl.multiple_of(start, LANES), LANES)]

    for level in range(FACTORS):
        for g in range(4):
            if level == 0:
                left = window(0, 2 * g * 1024 + half)
                right = window(0, (2 * g + 1) * 1024 + half)
                left = jnp.where(odd, pltpu.roll(left, 64, 1), left)
                right = jnp.where(odd, right, pltpu.roll(right, 64, 1))
                value = jnp.where(lane < 64, left, right)
            elif level == 1:
                value = window(1, g * 2048 + f * 128)
            elif level == 2:
                value = window(2, g // 2 * 4096 + f * 256 + g % 2 * LANES)
            else:
                value = window(3, f * 512 + g * LANES)
            sigma = (value >> (9 + level) & 1) * RUN + (value & (RUN - 1))
            idx_ref[level * 4 + g : level * 4 + g + 1, :] = sigma + lane // BLOCK * BLOCK

    for copy in copies:
        copy.wait()
    for h in range(8):
        rows8 = fetched[h * 8 : h * 8 + 8, :]
        pair = rows8[:2]
        for s in range(1, 4):
            pair = jnp.where(f % 4 == s, rows8[2 * s : 2 * s + 2], pair)
        chosen[2 * h : 2 * h + 2, :] = pair
    for g in range(4):
        rows8 = fetched[64 + g * 8 : 72 + g * 8, :]
        chosen[16 + 4 * g : 20 + 4 * g, :] = jnp.where(odd, rows8[4:], rows8[:4])
    chosen[32:96, :] = fetched[96:160, :]
    chosen[96:, :] = fetched[:32, :]
    turned[...] = chosen[...].T
    sub = iota((BLOCK, LANES), 0)
    for i in range(BLOCK):
        skew = turned[i * BLOCK : (i + 1) * BLOCK, :] - turned[pl.ds(i, BLOCK, stride=BLOCK), :]
        mat[i] = jnp.where(sub == i, 1.0, 0.0) - skew

    def step(pair, carry):
        k = 2 * pair
        here, next_here = sub == k, sub == k + 1
        either = here | next_here
        pivot = 1.0 / mat[k, pl.ds(k, 1), :]
        first = jnp.where(here, pivot, mat[k] * pivot)
        first_next = mat[k, pl.ds(k + 1, 1), :] * pivot
        factor = mat[k + 1, pl.ds(k, 1), :]
        second = jnp.where(here, 0.0, mat[k + 1]) - factor * first
        pivot = 1.0 / (mat[k + 1, pl.ds(k + 1, 1), :] - factor * first_next)
        second = jnp.where(next_here, pivot, second * pivot)
        cut = jnp.where(next_here, 0.0, first)
        for i in range(BLOCK):
            factor = mat[i, pl.ds(k, 1), :]
            after = mat[i, pl.ds(k + 1, 1), :] - factor * first_next
            mat[i] = jnp.where(either, 0.0, mat[i]) - factor * cut - after * second
        mat[k] = cut - first_next * second
        mat[k + 1] = second
        return carry

    lax.fori_loop(0, BLOCK // 2, step, 0)
    for i in range(BLOCK):
        rows[pl.ds(i, 96, stride=BLOCK), :] = mat[i].T[:96]
    same = iota((LANES, LANES), 0) // BLOCK == iota((LANES, LANES), 1) // BLOCK
    spread = jnp.where(iota((BLOCK, LANES), 0) == iota((BLOCK, LANES), 1) % BLOCK, 1.0, 0.0).astype(BF)
    unit = jnp.where(iota((LANES, BLOCK), 0) % BLOCK == iota((LANES, BLOCK), 1), 1.0, 0.0)
    for g in range(24):
        piece = rows[g * LANES : (g + 1) * LANES, :]
        if g < 16:
            rotation = dot((2.0 * piece - unit).astype(BF), spread, 1, 0)
            rotation = jnp.where(same, rotation, 0.0).astype(BF)
            rot_ref[g * LANES : (g + 1) * LANES, :] = dot(onehot(idx_ref, g), rotation, 1, 0).astype(BF)
        else:
            wide = jnp.where(same, jnp.concatenate([piece] * 4, axis=1), 0.0)
            inv_ref[(g - 16) * LANES : (g - 15) * LANES, :] = wide
    w_copy.wait()
    c_copy.wait()
    up_ref[...] = dot(w_ref[...], c_ref[...], 1, 1).astype(BF)


def onehot(idx_ref, g):
    return jnp.where(iota((LANES, LANES), 0) == idx_ref[g : g + 1, :], 1.0, 0.0).astype(BF)


def shuffle(x, level):
    groups = 16 >> level
    width = 512 // groups
    pieces = []
    for h in range(groups // 2):
        for i in range(width // RUN):
            for half in range(2):
                start = (2 * h + half) * width + i * RUN
                pieces.append(x[start : start + RUN])
    return jnp.concatenate(pieces, axis=0)


def unshuffle(x, level):
    groups = 16 >> level
    width = 512 // groups
    count = width // RUN
    pieces = []
    for a in range(groups):
        for i in range(count):
            start = ((a // 2) * count + i) * BLOCK + (a % 2) * RUN
            pieces.append(x[start : start + RUN])
    return jnp.concatenate(pieces, axis=0)


def forward_body(
    x_ref, rot_ref, weight, *rest, tiles
):
    parts, saved_ref = rest[:4], rest[4]
    w_ref, out_ref, staged, w_sems, p_sem = rest[5:]
    tile = weight.shape[1] // tiles
    fetches = []
    for i in range(tiles):
        span = pl.ds(i * tile, tile)
        fetches.append(pltpu.make_async_copy(weight.at[:, span], w_ref.at[:, span], w_sems.at[i]))
    for fetch in fetches:
        fetch.start()

    f = lax.axis_index("fsdp")
    z, x_own = f // 4, f % 4
    second = lax.axis_index("tensor") % 2 == 1
    x = x_ref[...]
    for level in range(FACTORS):
        x = shuffle(x, level)
        saved_ref[level] = x
        outs = []
        for g in range(4):
            rot = rot_ref[(level * 4 + g) * LANES : (level * 4 + g + 1) * LANES, :]
            mine = x[g * LANES : (g + 1) * LANES]
            if level < FACTORS - 1:
                outs.append(dot(rot, mine, 0, 0).astype(BF))
            else:
                outs.append(dot(mine, rot, 0, 0).astype(BF))
        x = jnp.concatenate(outs, axis=0 if level < FACTORS - 1 else 1)
    for block in range(16):
        dz, dx = (block // 4 - z + 4) % 4, (block % 4 - x_own + 4) % 4
        slot = jnp.where(second, dx * 4 + dz, dz * 4 + dx)
        out_ref[pl.ds(pl.multiple_of(slot * RUN, RUN), RUN), :] = x[block * RUN : (block + 1) * RUN]

    copies = []
    for i in range(tiles):
        span = pl.ds(i * tile, tile)
        fetches[i].wait()
        staged[i] = dot(out_ref[...], w_ref[:, span], 1, 0).astype(BF)
        for s in range(4):
            copy = pltpu.make_async_copy(staged.at[i, pl.ds(s * 64, 64)], parts[s].at[:, span], p_sem)
            copy.start()
            copies.append(copy)
    for copy in copies:
        copy.wait()


def forward(mixed, rot, weight, tiles=7):
    depth, tokens = mixed.shape
    columns = weight.shape[1]
    vmem = pl.BlockSpec(memory_space=pltpu.VMEM)
    hbm = pl.BlockSpec(memory_space=pltpu.HBM)
    return pl.pallas_call(
        functools.partial(forward_body, tiles=tiles),
        out_shape=[pltpu.HBM((tokens // 4, columns), BF)] * 4
        + [shape((FACTORS, depth, tokens), BF)],
        in_specs=[vmem, vmem, hbm],
        out_specs=[hbm] * 4 + [vmem],
        scratch_shapes=[
            pltpu.VMEM((depth, columns), BF),
            pltpu.VMEM((tokens, depth), BF),
            pltpu.VMEM((tiles, tokens, columns // tiles), BF),
            pltpu.SemaphoreType.DMA((tiles,)),
            pltpu.SemaphoreType.DMA,
        ],
        compiler_params=pltpu.CompilerParams(vmem_limit_bytes=32 << 20),
    )(mixed, rot, far(weight))


def backward_body(up_ref, saved_ref, rot_ref, idx_ref, grad_ref):
    d = lax.axis_index("dp")
    up = up_ref[...]
    same = iota((LANES, LANES), 0) // BLOCK == iota((LANES, LANES), 1) // BLOCK
    for level in reversed(range(FACTORS)):
        outs = []
        for g in range(4):
            base = (level * 4 + g) * LANES
            mine = up[g * LANES : (g + 1) * LANES]
            x = saved_ref[level, g * LANES : (g + 1) * LANES, :]
            moved = dot(onehot(idx_ref, level * 4 + g), x, 0, 0).astype(BF)
            outer = jnp.where(same, dot(moved, mine, 1, 1), 0.0)
            packed = outer[:BLOCK] + outer[BLOCK : 2 * BLOCK]
            packed = packed + outer[2 * BLOCK : 3 * BLOCK] + outer[3 * BLOCK :]
            grad_ref[(g // 2 + d) % 2, level, g % 2] = packed
            if level > 0:
                outs.append(dot(rot_ref[base : base + LANES, :], mine, 1, 0).astype(BF))
        if level > 0:
            up = unshuffle(jnp.concatenate(outs, axis=0), level)


def pull_body(g_ref, ad_ref, out_ref):
    same = iota((LANES, LANES), 0) // BLOCK == iota((LANES, LANES), 1) // BLOCK
    for g in range(8):
        grad = jnp.where(same, jnp.concatenate([g_ref[g]] * 4, axis=0), 0.0)
        inv = ad_ref[g * LANES : (g + 1) * LANES, :]
        both = 2.0 * dot(dot(inv, grad, 0, 0, HI), inv, 1, 1, HI)
        both = both - both.T
        packed = both[:BLOCK] + both[BLOCK : 2 * BLOCK]
        out_ref[g] = packed + both[2 * BLOCK : 3 * BLOCK] + both[3 * BLOCK :]


def ring_pairs(stage, s):
    pairs = []
    for f in range(16):
        for t in range(4):
            z, x = f // 4, f % 4
            if (t % 2) ^ stage:
                x = (x + s) % 4
            else:
                z = (z + s) % 4
            pairs.append((f * 4 + t, (z * 4 + x) * 4 + t))
    return pairs


def ring(x, stage, s):
    return lax.ppermute(x, ("fsdp", "tensor"), ring_pairs(stage, s))


def local(activations, frozen_weight, cayley_params, permutations, cotangent):
    tokens = activations.shape[0]
    mixed = lax.all_to_all(
        activations.T.reshape(16, BLOCK, tokens), "fsdp", 0, 0, tiled=True
    ).reshape(512, tokens)

    rot, inv, idx, up = pl.pallas_call(
        prepare_body,
        out_shape=(
            shape((2048, LANES), BF),
            shape((1024, LANES), F32),
            shape((16, LANES), jnp.int32),
            shape((512, tokens), BF),
        ),
        in_specs=[pl.BlockSpec(memory_space=pltpu.HBM)] * 4,
        out_specs=(pl.BlockSpec(memory_space=pltpu.VMEM),) * 4,
        scratch_shapes=[
            pltpu.VMEM(frozen_weight.shape, BF),
            pltpu.VMEM(cotangent.shape, BF),
            pltpu.VMEM((160, BLOCK * BLOCK), F32),
            pltpu.VMEM((LANES, BLOCK * BLOCK), F32),
            pltpu.VMEM((BLOCK * BLOCK, LANES), F32),
            pltpu.VMEM((BLOCK, BLOCK, LANES), F32),
            pltpu.VMEM((BLOCK * 96, BLOCK), F32),
            pltpu.VMEM((FACTORS, 8192), jnp.int32),
            pltpu.SemaphoreType.DMA,
            pltpu.SemaphoreType.DMA,
            pltpu.SemaphoreType.DMA,
            pltpu.SemaphoreType.DMA,
        ],
        compiler_params=pltpu.CompilerParams(vmem_limit_bytes=32 << 20),
    )(far(cayley_params), far(permutations), far(frozen_weight), far(cotangent))

    up, mixed = lax.optimization_barrier((up, mixed))
    *parts, saved = forward(mixed, rot, frozen_weight)
    near, back, across = [ring(parts[s], 0, s) for s in (1, 3, 2)]

    for bit in (1, 2):
        other = lax.ppermute(up, "tensor", [(t, t ^ bit) for t in range(4)])
        up = (up.astype(F32) + other).astype(BF)
    grads = call(
        backward_body, shape((2, FACTORS, 2, BLOCK, LANES), F32), (up, saved, rot, idx)
    )
    grads = grads[0] + lax.ppermute(grads[1], "dp", [(0, 1), (1, 0)])
    grads, across = lax.optimization_barrier((grads, across))

    f = lax.axis_index("fsdp")
    level3 = lax.ppermute(
        grads[3],
        ("dp", "fsdp"),
        [(e * 16 + s, s // 8 * 16 + s % 8 * 2 + e) for e in range(2) for s in range(16)],
    )
    spots = grads[0].reshape(2, BLOCK, 2, 64).transpose(0, 2, 1, 3).reshape(4, BLOCK, 64)
    odd = f % 2 == 1
    spots = jnp.concatenate([jnp.where(odd, 0.0, spots), jnp.where(odd, spots, 0.0)], axis=2)
    slots = jnp.stack([jnp.repeat(spots, 4, axis=0), jnp.repeat(grads[1], 8, axis=0)], axis=1)
    slots = lax.all_to_all(slots.astype(BF), "fsdp", 0, 0, tiled=True)

    near, level3 = lax.optimization_barrier((near, level3))
    parts = [parts[0], near, back, across]
    wide = [sum(p[k * RUN : (k + 1) * RUN].astype(F32) for p in parts).astype(BF) for k in range(4)]
    last = [ring(wide[s], 1, s) for s in (2, 1, 3)]

    level0 = lax.dynamic_slice_in_dim(slots[:, 0], f % 4 * 4, 4, 0).astype(F32)
    level0 = level0.reshape(2, 2, BLOCK, LANES).sum(1)
    level1 = lax.dynamic_slice_in_dim(slots[:, 1], f % 8 * 2, 2, 0).astype(F32)
    owned = jnp.concatenate([level0, level1, grads[2], level3], axis=0)
    pulled = call(pull_body, shape((8, BLOCK, LANES), F32), (owned, inv))
    param_grads = (
        pulled.reshape(FACTORS, 2, BLOCK, 4, BLOCK)
        .transpose(0, 1, 3, 2, 4)
        .reshape(FACTORS, 8, BLOCK * BLOCK)
    )
    param_grads, last = lax.optimization_barrier((param_grads, last))
    projected = sum(p.astype(F32) for p in [wide[0]] + last).astype(BF)
    return (projected, param_grads)


def solution(mesh):
    return jax.shard_map(
        local,
        mesh=mesh,
        in_specs=(P("dp", "fsdp"), P("fsdp", "tensor"), P(), P(), P("dp", "tensor")),
        out_specs=(P(("dp", "fsdp"), "tensor"), P(None, ("dp", "fsdp"), None)),
        check_vma=False,
    )
```

```python
import functools

import jax
import jax.numpy as jnp
from jax import lax
from jax.experimental import pallas as pl
from jax.experimental.pallas import tpu as pltpu
from jax.sharding import PartitionSpec as P

BLOCK = 32
FACTORS = 4
RUN = 16
LANES = 128
BF = jnp.bfloat16
F32 = jnp.float32
HI = lax.Precision.HIGHEST


def iota(shape, dim):
    return lax.broadcasted_iota(jnp.int32, shape, dim)


def dot(a, b, ca, cb, precision=None):
    return lax.dot_general(
        a, b, (((ca,), (cb,)), ((), ())), precision=precision, preferred_element_type=F32
    )


def call(body, out_shape, args, scratch=(), limit=12 << 20):
    return pl.pallas_call(
        body,
        out_shape=out_shape,
        in_specs=[pl.BlockSpec(memory_space=pltpu.VMEM)] * len(args),
        out_specs=jax.tree.map(lambda _: pl.BlockSpec(memory_space=pltpu.VMEM), out_shape),
        scratch_shapes=list(scratch),
        compiler_params=pltpu.CompilerParams(vmem_limit_bytes=limit),
    )(*args)


def shape(dims, dtype):
    return jax.ShapeDtypeStruct(dims, dtype)


def far(x):
    return pltpu.with_memory_space_constraint(x, pltpu.HBM)


def prepare_body(
    params,
    perms,
    weight,
    cotan,
    rot_ref,
    inv_ref,
    idx_ref,
    up_ref,
    w_ref,
    c_ref,
    fetched,
    chosen,
    turned,
    mat,
    rows,
    perm_ref,
    sem,
    perm_sem,
    w_sem,
    c_sem,
):
    f = lax.axis_index("fsdp")
    d = lax.axis_index("dp")
    copies = []

    def pull(level, start, count, to):
        source = params.at[level, pl.ds(pl.multiple_of(start, 8), count)]
        copies.append(pltpu.make_async_copy(source, fetched.at[pl.ds(to, count)], sem))

    for h in range(8):
        pull(0, h * 32 + f // 4 * 8, 8, h * 8)
    for g in range(4):
        pull(1, g * 64 + f // 2 * 8, 8, 64 + g * 8)
    for g in range(2):
        pull(2, g * 128 + f * 8, 8, 96 + g * 8)
    pull(3, f * 16, 16, 112)
    for level in range(FACTORS):
        pull(level, (d * 16 + f) * 8, 8, 128 + level * 8)
    for copy in copies:
        copy.start()
    perm_copy = pltpu.make_async_copy(perms, perm_ref, perm_sem)
    perm_copy.start()
    w_copy = pltpu.make_async_copy(weight, w_ref, w_sem)
    w_copy.start()
    c_copy = pltpu.make_async_copy(cotan, c_ref, c_sem)
    c_copy.start()
    perm_copy.wait()

    lane = iota((1, LANES), 1)
    odd = f % 2 == 1
    half = f // 2 * LANES

    def window(level, start):
        return perm_ref[level : level + 1, pl.ds(pl.multiple_of(start, LANES), LANES)]

    for level in range(FACTORS):
        for g in range(4):
            if level == 0:
                left = window(0, 2 * g * 1024 + half)
                right = window(0, (2 * g + 1) * 1024 + half)
                left = jnp.where(odd, pltpu.roll(left, 64, 1), left)
                right = jnp.where(odd, right, pltpu.roll(right, 64, 1))
                value = jnp.where(lane < 64, left, right)
            elif level == 1:
                value = window(1, g * 2048 + f * 128)
            elif level == 2:
                value = window(2, g // 2 * 4096 + f * 256 + g % 2 * LANES)
            else:
                value = window(3, f * 512 + g * LANES)
            sigma = (value >> (9 + level) & 1) * RUN + (value & (RUN - 1))
            idx_ref[level * 4 + g : level * 4 + g + 1, :] = sigma + lane // BLOCK * BLOCK

    for copy in copies:
        copy.wait()
    for h in range(8):
        rows8 = fetched[h * 8 : h * 8 + 8, :]
        pair = rows8[:2]
        for s in range(1, 4):
            pair = jnp.where(f % 4 == s, rows8[2 * s : 2 * s + 2], pair)
        chosen[2 * h : 2 * h + 2, :] = pair
    for g in range(4):
        rows8 = fetched[64 + g * 8 : 72 + g * 8, :]
        chosen[16 + 4 * g : 20 + 4 * g, :] = jnp.where(odd, rows8[4:], rows8[:4])
    chosen[32:96, :] = fetched[96:160, :]
    chosen[96:, :] = fetched[:32, :]
    turned[...] = chosen[...].T
    sub = iota((BLOCK, LANES), 0)
    for i in range(BLOCK):
        skew = turned[i * BLOCK : (i + 1) * BLOCK, :] - turned[pl.ds(i, BLOCK, stride=BLOCK), :]
        mat[i] = jnp.where(sub == i, 1.0, 0.0) - skew

    def step(pair, carry):
        k = 2 * pair
        here, next_here = sub == k, sub == k + 1
        either = here | next_here
        pivot = 1.0 / mat[k, pl.ds(k, 1), :]
        first = jnp.where(here, pivot, mat[k] * pivot)
        first_next = mat[k, pl.ds(k + 1, 1), :] * pivot
        factor = mat[k + 1, pl.ds(k, 1), :]
        second = jnp.where(here, 0.0, mat[k + 1]) - factor * first
        pivot = 1.0 / (mat[k + 1, pl.ds(k + 1, 1), :] - factor * first_next)
        second = jnp.where(next_here, pivot, second * pivot)
        cut = jnp.where(next_here, 0.0, first)
        for i in range(BLOCK):
            factor = mat[i, pl.ds(k, 1), :]
            after = mat[i, pl.ds(k + 1, 1), :] - factor * first_next
            mat[i] = jnp.where(either, 0.0, mat[i]) - factor * cut - after * second
        mat[k] = cut - first_next * second
        mat[k + 1] = second
        return carry

    lax.fori_loop(0, BLOCK // 2, step, 0)
    for i in range(BLOCK):
        rows[pl.ds(i, 96, stride=BLOCK), :] = mat[i].T[:96]
    same = iota((LANES, LANES), 0) // BLOCK == iota((LANES, LANES), 1) // BLOCK
    spread = jnp.where(iota((BLOCK, LANES), 0) == iota((BLOCK, LANES), 1) % BLOCK, 1.0, 0.0).astype(BF)
    unit = jnp.where(iota((LANES, BLOCK), 0) % BLOCK == iota((LANES, BLOCK), 1), 1.0, 0.0)
    for g in range(24):
        piece = rows[g * LANES : (g + 1) * LANES, :]
        if g < 16:
            rotation = dot((2.0 * piece - unit).astype(BF), spread, 1, 0)
            rotation = jnp.where(same, rotation, 0.0).astype(BF)
            rot_ref[g * LANES : (g + 1) * LANES, :] = dot(onehot(idx_ref, g), rotation, 1, 0).astype(BF)
        else:
            wide = jnp.where(same, jnp.concatenate([piece] * 4, axis=1), 0.0)
            inv_ref[(g - 16) * LANES : (g - 15) * LANES, :] = wide
    w_copy.wait()
    c_copy.wait()
    up_ref[...] = dot(w_ref[...], c_ref[...], 1, 1).astype(BF)


def onehot(idx_ref, g):
    return jnp.where(iota((LANES, LANES), 0) == idx_ref[g : g + 1, :], 1.0, 0.0).astype(BF)


def shuffle(x, level):
    groups = 16 >> level
    width = 512 // groups
    pieces = []
    for h in range(groups // 2):
        for i in range(width // RUN):
            for half in range(2):
                start = (2 * h + half) * width + i * RUN
                pieces.append(x[start : start + RUN])
    return jnp.concatenate(pieces, axis=0)


def unshuffle(x, level):
    groups = 16 >> level
    width = 512 // groups
    count = width // RUN
    pieces = []
    for a in range(groups):
        for i in range(count):
            start = ((a // 2) * count + i) * BLOCK + (a % 2) * RUN
            pieces.append(x[start : start + RUN])
    return jnp.concatenate(pieces, axis=0)


def forward_body(
    x_ref, rot_ref, weight, *rest, tiles
):
    parts, saved_ref = rest[:4], rest[4]
    w_ref, out_ref, staged, w_sems, p_sem = rest[5:]
    tile = weight.shape[1] // tiles
    fetches = []
    for i in range(tiles):
        span = pl.ds(i * tile, tile)
        fetches.append(pltpu.make_async_copy(weight.at[:, span], w_ref.at[:, span], w_sems.at[i]))
    for fetch in fetches:
        fetch.start()

    f = lax.axis_index("fsdp")
    z, x_own = f // 4, f % 4
    second = lax.axis_index("tensor") % 2 == 1
    x = x_ref[...]
    for level in range(FACTORS):
        x = shuffle(x, level)
        saved_ref[level] = x
        outs = []
        for g in range(4):
            rot = rot_ref[(level * 4 + g) * LANES : (level * 4 + g + 1) * LANES, :]
            mine = x[g * LANES : (g + 1) * LANES]
            if level < FACTORS - 1:
                outs.append(dot(rot, mine, 0, 0).astype(BF))
            else:
                outs.append(dot(mine, rot, 0, 0).astype(BF))
        x = jnp.concatenate(outs, axis=0 if level < FACTORS - 1 else 1)
    for block in range(16):
        dz, dx = (block // 4 - z + 4) % 4, (block % 4 - x_own + 4) % 4
        slot = jnp.where(second, dx * 4 + dz, dz * 4 + dx)
        out_ref[pl.ds(pl.multiple_of(slot * RUN, RUN), RUN), :] = x[block * RUN : (block + 1) * RUN]

    copies = []
    for i in range(tiles):
        span = pl.ds(i * tile, tile)
        fetches[i].wait()
        staged[i] = dot(out_ref[...], w_ref[:, span], 1, 0).astype(BF)
        for s in range(4):
            copy = pltpu.make_async_copy(staged.at[i, pl.ds(s * 64, 64)], parts[s].at[:, span], p_sem)
            copy.start()
            copies.append(copy)
    for copy in copies:
        copy.wait()


def forward(mixed, rot, weight, tiles=4):
    depth, tokens = mixed.shape
    columns = weight.shape[1]
    vmem = pl.BlockSpec(memory_space=pltpu.VMEM)
    hbm = pl.BlockSpec(memory_space=pltpu.HBM)
    return pl.pallas_call(
        functools.partial(forward_body, tiles=tiles),
        out_shape=[pltpu.HBM((tokens // 4, columns), BF)] * 4
        + [shape((FACTORS, depth, tokens), BF)],
        in_specs=[vmem, vmem, hbm],
        out_specs=[hbm] * 4 + [vmem],
        scratch_shapes=[
            pltpu.VMEM((depth, columns), BF),
            pltpu.VMEM((tokens, depth), BF),
            pltpu.VMEM((tiles, tokens, columns // tiles), BF),
            pltpu.SemaphoreType.DMA((tiles,)),
            pltpu.SemaphoreType.DMA,
        ],
        compiler_params=pltpu.CompilerParams(vmem_limit_bytes=32 << 20),
    )(mixed, rot, far(weight))


def backward_body(up_ref, saved_ref, rot_ref, idx_ref, grad_ref):
    d = lax.axis_index("dp")
    up = up_ref[...]
    same = iota((LANES, LANES), 0) // BLOCK == iota((LANES, LANES), 1) // BLOCK
    for level in reversed(range(FACTORS)):
        outs = []
        for g in range(4):
            base = (level * 4 + g) * LANES
            mine = up[g * LANES : (g + 1) * LANES]
            x = saved_ref[level, g * LANES : (g + 1) * LANES, :]
            moved = dot(onehot(idx_ref, level * 4 + g), x, 0, 0).astype(BF)
            outer = jnp.where(same, dot(moved, mine, 1, 1), 0.0)
            packed = outer[:BLOCK] + outer[BLOCK : 2 * BLOCK]
            packed = packed + outer[2 * BLOCK : 3 * BLOCK] + outer[3 * BLOCK :]
            grad_ref[(g // 2 + d) % 2, level, g % 2] = packed
            if level > 0:
                outs.append(dot(rot_ref[base : base + LANES, :], mine, 1, 0).astype(BF))
        if level > 0:
            up = unshuffle(jnp.concatenate(outs, axis=0), level)


def pull_body(g_ref, ad_ref, out_ref):
    same = iota((LANES, LANES), 0) // BLOCK == iota((LANES, LANES), 1) // BLOCK
    for g in range(8):
        grad = jnp.where(same, jnp.concatenate([g_ref[g]] * 4, axis=0), 0.0)
        inv = ad_ref[g * LANES : (g + 1) * LANES, :]
        both = 2.0 * dot(dot(inv, grad, 0, 0, HI), inv, 1, 1, HI)
        both = both - both.T
        packed = both[:BLOCK] + both[BLOCK : 2 * BLOCK]
        out_ref[g] = packed + both[2 * BLOCK : 3 * BLOCK] + both[3 * BLOCK :]


def ring_pairs(stage, s):
    pairs = []
    for f in range(16):
        for t in range(4):
            z, x = f // 4, f % 4
            if (t % 2) ^ stage:
                x = (x + s) % 4
            else:
                z = (z + s) % 4
            pairs.append((f * 4 + t, (z * 4 + x) * 4 + t))
    return pairs


def ring(x, stage, s):
    return lax.ppermute(x, ("fsdp", "tensor"), ring_pairs(stage, s))


def local(activations, frozen_weight, cayley_params, permutations, cotangent):
    tokens = activations.shape[0]
    mixed = lax.all_to_all(
        activations.T.reshape(16, BLOCK, tokens), "fsdp", 0, 0, tiled=True
    ).reshape(512, tokens)

    rot, inv, idx, up = pl.pallas_call(
        prepare_body,
        out_shape=(
            shape((2048, LANES), BF),
            shape((1024, LANES), F32),
            shape((16, LANES), jnp.int32),
            shape((512, tokens), BF),
        ),
        in_specs=[pl.BlockSpec(memory_space=pltpu.HBM)] * 4,
        out_specs=(pl.BlockSpec(memory_space=pltpu.VMEM),) * 4,
        scratch_shapes=[
            pltpu.VMEM(frozen_weight.shape, BF),
            pltpu.VMEM(cotangent.shape, BF),
            pltpu.VMEM((160, BLOCK * BLOCK), F32),
            pltpu.VMEM((LANES, BLOCK * BLOCK), F32),
            pltpu.VMEM((BLOCK * BLOCK, LANES), F32),
            pltpu.VMEM((BLOCK, BLOCK, LANES), F32),
            pltpu.VMEM((BLOCK * 96, BLOCK), F32),
            pltpu.VMEM((FACTORS, 8192), jnp.int32),
            pltpu.SemaphoreType.DMA,
            pltpu.SemaphoreType.DMA,
            pltpu.SemaphoreType.DMA,
            pltpu.SemaphoreType.DMA,
        ],
        compiler_params=pltpu.CompilerParams(vmem_limit_bytes=32 << 20),
    )(far(cayley_params), far(permutations), far(frozen_weight), far(cotangent))

    up, mixed = lax.optimization_barrier((up, mixed))
    *parts, saved = forward(mixed, rot, frozen_weight)
    near, back, across = [ring(parts[s], 0, s) for s in (1, 3, 2)]

    for bit in (1, 2):
        other = lax.ppermute(up, "tensor", [(t, t ^ bit) for t in range(4)])
        up = (up.astype(F32) + other).astype(BF)
    grads = call(
        backward_body, shape((2, FACTORS, 2, BLOCK, LANES), F32), (up, saved, rot, idx)
    )
    grads = grads[0] + lax.ppermute(grads[1], "dp", [(0, 1), (1, 0)])
    grads, across = lax.optimization_barrier((grads, across))

    f = lax.axis_index("fsdp")
    level3 = lax.ppermute(
        grads[3],
        ("dp", "fsdp"),
        [(e * 16 + s, s // 8 * 16 + s % 8 * 2 + e) for e in range(2) for s in range(16)],
    )
    spots = grads[0].reshape(2, BLOCK, 2, 64).transpose(0, 2, 1, 3).reshape(4, BLOCK, 64)
    odd = f % 2 == 1
    spots = jnp.concatenate([jnp.where(odd, 0.0, spots), jnp.where(odd, spots, 0.0)], axis=2)
    slots = jnp.stack([jnp.repeat(spots, 4, axis=0), jnp.repeat(grads[1], 8, axis=0)], axis=1)
    slots = lax.all_to_all(slots.astype(BF), "fsdp", 0, 0, tiled=True)

    near, level3 = lax.optimization_barrier((near, level3))
    parts = [parts[0], near, back, across]
    wide = [sum(p[k * RUN : (k + 1) * RUN].astype(F32) for p in parts).astype(BF) for k in range(4)]
    last = [ring(wide[s], 1, s) for s in (2, 1, 3)]

    level0 = lax.dynamic_slice_in_dim(slots[:, 0], f % 4 * 4, 4, 0).astype(F32)
    level0 = level0.reshape(2, 2, BLOCK, LANES).sum(1)
    level1 = lax.dynamic_slice_in_dim(slots[:, 1], f % 8 * 2, 2, 0).astype(F32)
    owned = jnp.concatenate([level0, level1, grads[2], level3], axis=0)
    pulled = call(pull_body, shape((8, BLOCK, LANES), F32), (owned, inv))
    param_grads = (
        pulled.reshape(FACTORS, 2, BLOCK, 4, BLOCK)
        .transpose(0, 1, 3, 2, 4)
        .reshape(FACTORS, 8, BLOCK * BLOCK)
    )
    param_grads, last = lax.optimization_barrier((param_grads, last))
    projected = sum(p.astype(F32) for p in [wide[0]] + last).astype(BF)
    return (projected, param_grads)


def solution(mesh):
    return jax.shard_map(
        local,
        mesh=mesh,
        in_specs=(P("dp", "fsdp"), P("fsdp", "tensor"), P(), P(), P("dp", "tensor")),
        out_specs=(P(("dp", "fsdp"), "tensor"), P(None, ("dp", "fsdp"), None)),
        check_vma=False,
    )
```
